32 devices in a mesh: sec: 16 (over z, y, x), blk: 2 (over core).
Axes of the slice: x: 2, y: 2, z: 4, core: 2. Of those that a mesh axis runs over, the one named last changes fastest.
Arguments:
- slab_state: float32 [9, 8, 256, 256], P(None, None, 'sec', 'blk'), may hold values from -6 to 6
- buoyancy: float32 [8, 256, 256], P(None, 'sec', 'blk'), may hold values from 0.5 to 1
- lame_lambda: float32 [8, 256, 256], P(None, 'sec', 'blk'), may hold values from 0.5 to 2
- lame_mu: float32 [8, 256, 256], P(None, 'sec', 'blk'), may hold values from 0.3 to 1.2
- face_map: int32 [256], replicated, may hold values from 0 to 1023
- band_widths: int32 [16, 2], P('sec'), may hold values from 2 to 9
- ocean_state: float32 [3, 256, 1024], P(None, 'sec', 'blk'), may hold values from -6 to 6
- water_depth: float32 [256, 1024], P('sec', 'blk'), may hold values from 0.25 to 1
Outputs:
- slab_out: float32 [9, 8, 256, 256], P(None, None, 'sec', 'blk')
- ocean_out: float32 [3, 256, 1024], P(None, 'sec', 'blk')
The draws below stay inside these ranges and needn't reach their ends.
Inputs may be any that keep to these rules, and one draw needn't show every extreme that they name: `face_map`: each entry is the ocean column over which that seafloor face column lies. `band_widths`: the Kajiura band width of each ocean tile in ocean cells.
All inputs are finite; a program needn't handle non-finite values.
Results may differ from the reference program's by a relative error of at most 0.00014.
Values sent between devices are 32-bit elements; how exact they have to be, the bound alone decides.
A program may use at most 64 MiB of HBM per device.

```python
import math
import jax
import jax.numpy as jnp
import numpy as np
from jax import lax

THICKNESS = 8
STRIKE_DEV = 16
OCEAN_DEV = 512
FIELDS = 9
SLAB_STEPS = 2
WAVE_STEPS = 4
STRIKE = 256
DIP = 256
OCEAN_COLS = 1024
TILE_ROWS = 16
TILE_COLS = 2
N_SEC = 16


def touch_ends(result, own_key, smallest, top_value):
    longest = result.shape.index(max(result.shape))
    spots = []
    for shift in (0, 1):
        where = [jax.random.randint(jax.random.fold_in(own_key, axis), (), 0, length) for axis, length in enumerate(result.shape)]
        where[longest] = (where[longest] + shift) % result.shape[longest]
        spots.append(tuple(where))
    return result.at[spots[0]].set(smallest).at[spots[1]].set(top_value)


def block_scale(stream_key, dims, pieces, low, largest):
    def one(axis_at, parts):
        draws = jax.random.uniform(jax.random.fold_in(jax.random.fold_in(stream_key, 6), axis_at), (parts,), jnp.float32, low / len(pieces), largest / len(pieces))
        return jnp.repeat(jnp.exp(draws), dims[axis_at] // parts).reshape((-1,) + (1,) * (len(dims) - axis_at - 1))

    gain = one(*pieces[0])
    for cut in pieces[1:]:
        gain = gain * one(*cut)
    return gain


def rank_table(amount, skew):
    loads = [(1 << 20) // math.isqrt(rank ** skew) + 1 for rank in range(1, amount + 1)]
    width = 1 + sum(loads) // (1 << 30)
    return np.cumsum(np.array([max(1, weight // width) for weight in loads]))


def ranked_ids(rng, shape, amount, skew):
    listing = rank_table(amount, skew)
    ticket = jax.random.randint(jax.random.fold_in(rng, 1), shape, 0, int(listing[amount - 1]))
    rank = jnp.searchsorted(jnp.asarray(listing, jnp.int32), ticket, side="right")
    return jax.random.permutation(jax.random.fold_in(rng, 2), amount)[rank].astype(jnp.int32)


def gaussian(stream_key, dims, deviation, limit, pieces=(), kind=jnp.bfloat16):
    gain = block_scale(stream_key, dims, pieces, -0.22, 0.18) if pieces else 1.0
    values = jax.random.normal(stream_key, dims, jnp.float32) * deviation * gain
    return jnp.minimum(jnp.maximum(values, -limit), limit).astype(kind)


def setup_inputs(seed: int = 0) -> dict:
    streams_of = jax.random.split(jax.random.key(seed), 9)
    slab_state = gaussian(streams_of[0], (FIELDS, THICKNESS, STRIKE, DIP), 1.0, 6.0, ((2, 16), (3, 2)), jnp.float32)
    buoyancy = jnp.clip(jnp.exp(math.log(1.0) - 0.6931472 * jax.random.uniform(streams_of[1], (THICKNESS, STRIKE, DIP), jnp.float32) ** block_scale(streams_of[1], (THICKNESS, STRIKE, DIP), ((1, 16), (2, 2)), -0.2, 0.2)), 0.5, 1.0)
    lame_lambda = jnp.clip(jnp.exp(math.log(2.0) - 1.3862944 * jax.random.uniform(streams_of[2], (THICKNESS, STRIKE, DIP), jnp.float32) ** block_scale(streams_of[2], (THICKNESS, STRIKE, DIP), ((1, 16), (2, 2)), -0.2, 0.2)), 0.5, 2.0)
    lame_mu = jnp.clip(jnp.exp(math.log(1.2) - 1.3862944 * jax.random.uniform(streams_of[3], (THICKNESS, STRIKE, DIP), jnp.float32) ** block_scale(streams_of[3], (THICKNESS, STRIKE, DIP), ((1, 16), (2, 2)), -0.2, 0.2)), 0.3, 1.2)
    face_map = touch_ends(ranked_ids(streams_of[4], (DIP,), OCEAN_COLS, 2), jax.random.fold_in(streams_of[4], 3), 0, OCEAN_COLS - 1).astype(jnp.int32)
    band_widths = touch_ends(jax.random.randint(streams_of[5], (TILE_ROWS, TILE_COLS), 2, 10), jax.random.fold_in(streams_of[5], 1), 2, 9).astype(jnp.int32)
    ocean_state = gaussian(streams_of[6], (3, STRIKE, OCEAN_COLS), 1.0, 6.0, ((1, 16), (2, 2)), jnp.float32)
    water_depth = jnp.clip(jnp.exp(math.log(1.0) - 1.3862944 * jax.random.uniform(streams_of[7], (STRIKE, OCEAN_COLS), jnp.float32) ** block_scale(streams_of[7], (STRIKE, OCEAN_COLS), ((0, 16), (1, 2)), -0.2, 0.2)), 0.25, 1.0)
    return {"slab_state": slab_state, "buoyancy": buoyancy, "lame_lambda": lame_lambda, "lame_mu": lame_mu, "face_map": face_map, "band_widths": band_widths, "ocean_state": ocean_state, "water_depth": water_depth}


time_step = 0.25
wave_step = 0.5


def sech_kernel(distance, band_width):
    scaled = jnp.abs(distance) * (math.pi / 2.0) / band_width
    decay = jnp.exp(-scaled)
    return 2.0 * decay / (1.0 + decay * decay) / (2.0 * band_width)


def offset_slice(values, dimension, offset):
    slicer = [slice(1, -1)] * 3
    extent = values.shape[dimension]
    slicer[dimension] = slice(1 + offset, extent - 1 + offset)
    return values[tuple(slicer)]


def forward(values, dimension):
    return offset_slice(values, dimension, 1) - offset_slice(values, dimension, 0)


def backward(values, dimension):
    return offset_slice(values, dimension, 0) - offset_slice(values, dimension, -1)


def new_velocity(velocity, stress_padded, buoyancy):
    results = []
    for dimension in range(3):
        summed = forward(stress_padded[dimension], dimension)
        for across in range(3):
            if across != dimension:
                summed = summed + backward(stress_padded[6 - dimension - across], across)
        results.append(velocity[dimension] + time_step * buoyancy * summed)
    return jnp.stack(results)


def new_stress(stress, velocity_padded, lame_lambda, lame_mu):
    strain_rates = [backward(velocity_padded[dimension], dimension) for dimension in range(3)]
    dilatation = strain_rates[0] + strain_rates[1] + strain_rates[2]
    results = []
    for dimension in range(3):
        results.append(stress[dimension] + time_step * (lame_lambda * dilatation + 2.0 * lame_mu * strain_rates[dimension]))
    results.append(stress[3] + time_step * lame_mu * (forward(velocity_padded[1], 2) + forward(velocity_padded[2], 1)))
    results.append(stress[4] + time_step * lame_mu * (forward(velocity_padded[0], 2) + forward(velocity_padded[2], 0)))
    results.append(stress[5] + time_step * lame_mu * (forward(velocity_padded[0], 1) + forward(velocity_padded[1], 0)))
    return jnp.stack(results)


def pad_all(values):
    return jnp.pad(values, ((0, 0), (1, 1), (1, 1), (1, 1)))


def reference(slab_state, buoyancy, lame_lambda, lame_mu, face_map, band_widths, ocean_state, water_depth):
    velocity = slab_state[:3]
    stress = slab_state[3:]
    surface_rate = jnp.zeros(slab_state.shape[2:], jnp.float32)
    for stepping in range(SLAB_STEPS):
        velocity = new_velocity(velocity, pad_all(stress), buoyancy)
        surface_rate = surface_rate + velocity[0, 0]
        stress = new_stress(stress, pad_all(velocity), lame_lambda, lame_mu)
    slab_out = jnp.concatenate([velocity, stress], 0)
    uplift = time_step * surface_rate
    columns = jnp.arange(OCEAN_COLS, dtype=jnp.int32)

    def section_source(section):
        strip_rows = lax.dynamic_slice_in_dim(uplift, section * STRIKE_DEV, STRIKE_DEV, 0)
        tile_bands = lax.dynamic_index_in_dim(band_widths, section, 0, keepdims=False)
        widths = jnp.repeat(tile_bands, OCEAN_DEV).astype(jnp.float32)
        distance = (columns[:, None] - face_map[None, :]).astype(jnp.float32)
        kernel = sech_kernel(distance, widths[:, None])
        return jnp.einsum("xy,cy->xc", strip_rows, kernel, precision=lax.Precision.HIGHEST)

    source = lax.map(section_source, jnp.arange(N_SEC, dtype=jnp.int32)).reshape(STRIKE, OCEAN_COLS)
    surface = ocean_state[0] + source
    flux_strike = ocean_state[1]
    flux_dip = ocean_state[2]
    for stepping in range(WAVE_STEPS):
        padded_strike = jnp.pad(flux_strike, 1)
        padded_dip = jnp.pad(flux_dip, 1)
        surface = surface - wave_step * 0.5 * ((padded_strike[2:, 1:-1] - padded_strike[:-2, 1:-1]) + (padded_dip[1:-1, 2:] - padded_dip[1:-1, :-2]))
        padded_surface = jnp.pad(surface, 1)
        flux_strike = flux_strike - wave_step * 0.5 * water_depth * (padded_surface[2:, 1:-1] - padded_surface[:-2, 1:-1])
        flux_dip = flux_dip - wave_step * 0.5 * water_depth * (padded_surface[1:-1, 2:] - padded_surface[1:-1, :-2])
    ocean_out = jnp.stack([surface, flux_strike, flux_dip])
    return slab_out, ocean_out
```

```python
import functools
import math

import jax
import jax.numpy as jnp
from jax import lax
from jax.experimental import pallas as pl
from jax.experimental.pallas import tpu as pltpu
from jax.sharding import PartitionSpec as P

MESH = pl.DeviceIdType.MESH
WAVE_STEPS = 4
time_step = 0.25
wave_step = 0.5

V1, V2, V3, S11, S22, S33, S23, S13, S12, BUO, LAM, MU = range(12)
FIELDS = 9
ALL = 12
HALO = 2
OHALO = 8
FRONT = 3

SEC_DIRS = (1, -1)


def rows_up(x):
    return pltpu.roll(x, x.shape[0] - 1, 0)


def rows_down(x):
    return pltpu.roll(x, 1, 0)


def lanes_up(x):
    return pltpu.roll(x, x.shape[1] - 1, 1)


def lanes_down(x):
    return pltpu.roll(x, 1, 1)


def kernel_body(
    slab, buoyancy, lame_lambda, lame_mu, face_map, bands, ocean, depth,
    slab_out, ocean_out,
    ext, send_rows, recv_rows, pack, recv_pack, send_corner, recv_corner, ext_pack,
    oext, opack, recv_opack, recv_ocorner, wown, wrecv, uplift, k_hi, k_lo,
    sec_send, sec_recv, blk_send, blk_recv, diag_send, diag_recv, up_send, up_recv,
):
    n_sec = lax.axis_size("sec")
    n_blk = lax.axis_size("blk")
    sec = lax.axis_index("sec")
    blk = lax.axis_index("blk")
    thick, rows, lanes = slab.shape[1:]
    ext_rows = ext.shape[2]
    ocols = ocean.shape[2]
    oext_cols = oext.shape[2]
    tile_cols = bands.shape[1]

    def has_sec(step):
        return sec + step < n_sec if step > 0 else sec + step >= 0

    def has_blk(step):
        return blk + step < n_blk if step > 0 else blk + step >= 0

    recv_rows[...] = jnp.zeros_like(recv_rows)
    recv_pack[...] = jnp.zeros_like(recv_pack)
    recv_corner[...] = jnp.zeros_like(recv_corner)
    recv_opack[...] = jnp.zeros_like(recv_opack)
    recv_ocorner[...] = jnp.zeros_like(recv_ocorner)
    wrecv[...] = jnp.ones_like(wrecv)
    uplift[:, 0:OHALO, :] = jnp.zeros((n_blk, OHALO, lanes), jnp.float32)
    uplift[:, OHALO + rows:, :] = jnp.zeros((n_blk, OHALO, lanes), jnp.float32)
    oext[:, 0:OHALO, 0:ocols] = jnp.zeros((4, OHALO, ocols), jnp.float32)
    oext[:, OHALO + rows:, 0:ocols] = jnp.zeros((4, OHALO, ocols), jnp.float32)

    barrier = pltpu.get_barrier_semaphore()

    def greet(step, turn):
        pl.semaphore_signal(
            barrier, inc=1,
            device_id=(sec + step, lax.rem(blk + turn, n_blk)), device_id_type=MESH,
        )

    for turn in range(1, n_blk):
        greet(0, turn)
    for step in SEC_DIRS:
        @pl.when(has_sec(step))
        def _():
            for turn in range(n_blk):
                greet(step, turn)

    lane = lax.broadcasted_iota(jnp.int32, (rows, lanes), 1)
    sources = [(slab, f) for f in range(FIELDS)] + [
        (buoyancy, None), (lame_lambda, None), (lame_mu, None)]

    def pack_layer(t, carry):
        packed = jnp.zeros((rows, lanes), jnp.float32)
        for f, (ref, at) in enumerate(sources):
            value = ref[t] if at is None else ref[at, t]
            ext[f, t + 1, 0:rows, 0:lanes] = value
            send_rows[0, t, HALO * f:HALO * f + HALO, :] = value[rows - HALO:, :]
            send_rows[1, t, HALO * f:HALO * f + HALO, :] = value[0:HALO, :]
            moved = pltpu.roll(value, 4 * f, 1) if f else value
            packed = jnp.where(((lane - 4 * f + 2) & (lanes - 1)) < 4, moved, packed)
        pack[t] = packed
        send_corner[0, t] = packed[rows - HALO:, :]
        send_corner[1, t] = packed[0:HALO, :]
        return carry

    lax.fori_loop(0, thick, pack_layer, 0)

    opacked = jnp.zeros((rows, lanes), jnp.float32)
    for a in range(4):
        value = ocean[a] if a < 3 else depth[...]
        oext[a, OHALO:OHALO + rows, 0:ocols] = value
        edges = jnp.where(lane < lanes // 2, value[:, 0:lanes], value[:, ocols - lanes:])
        moved = pltpu.roll(edges, 16 * a, 1) if a else edges
        opacked = jnp.where(((lane - 16 * a + 8) & (lanes - 1)) < 16, moved, opacked)
    opack[...] = opacked

    wlane = lax.broadcasted_iota(jnp.int32, wown.shape, 1)
    wvalue = jnp.ones(wown.shape, jnp.float32)
    for j in range(tile_cols):
        wvalue = jnp.where(wlane == j, bands[0:1, j:j + 1].astype(jnp.float32), wvalue)
    wown[...] = wvalue

    near = (n_blk - 1) + sum(
        jnp.where(has_sec(step), n_blk, 0) for step in SEC_DIRS)
    pl.semaphore_wait(barrier, near)

    def sec_copies(d):
        step = SEC_DIRS[d]
        target = (sec + step, blk)
        own_rows = pl.ds(OHALO + rows - OHALO, OHALO) if d == 0 else pl.ds(OHALO, OHALO)
        to_rows = pl.ds(0, OHALO) if d == 0 else pl.ds(OHALO + rows, OHALO)
        pairs = [
            (send_rows.at[d, pl.ds(0, FRONT)], recv_rows.at[d, pl.ds(0, FRONT)]),
            (wown, wrecv.at[d]),
            (send_rows.at[d, pl.ds(FRONT, thick - FRONT)],
             recv_rows.at[d, pl.ds(FRONT, thick - FRONT)]),
            (oext.at[:, own_rows, pl.ds(0, ocols)], oext.at[:, to_rows, pl.ds(0, ocols)]),
        ]
        return [
            pltpu.make_async_remote_copy(
                src_ref=src, dst_ref=dst, send_sem=sec_send.at[d, i], recv_sem=sec_recv.at[d, i],
                device_id=target, device_id_type=MESH)
            for i, (src, dst) in enumerate(pairs)
        ]

    def blk_copies(e):
        target = (sec, blk + SEC_DIRS[e])
        pairs = [(pack, recv_pack.at[e]), (opack, recv_opack.at[e])]
        return [
            pltpu.make_async_remote_copy(
                src_ref=src, dst_ref=dst, send_sem=blk_send.at[e, i], recv_sem=blk_recv.at[e, i],
                device_id=target, device_id_type=MESH)
            for i, (src, dst) in enumerate(pairs)
        ]

    def diag_copies(d, e):
        target = (sec + SEC_DIRS[d], blk + SEC_DIRS[e])
        orows = pl.ds(rows - OHALO, OHALO) if d == 0 else pl.ds(0, OHALO)
        pairs = [
            (send_corner.at[d], recv_corner.at[d, e]),
            (opack.at[orows], recv_ocorner.at[d, e]),
        ]
        return [
            pltpu.make_async_remote_copy(
                src_ref=src, dst_ref=dst, send_sem=diag_send.at[d, e, i],
                recv_sem=diag_recv.at[d, e, i], device_id=target, device_id_type=MESH)
            for i, (src, dst) in enumerate(pairs)
        ]

    def both(d, e):
        return jnp.logical_and(has_sec(SEC_DIRS[d]), has_blk(SEC_DIRS[e]))

    def from_both(d, e):
        return jnp.logical_and(has_sec(-SEC_DIRS[d]), has_blk(-SEC_DIRS[e]))

    def start_at(condition, copies, i):
        @pl.when(condition)
        def _():
            copies[i].start()

    for i in (0,):
        for d in range(2):
            start_at(has_sec(SEC_DIRS[d]), sec_copies(d), 0)
        for d in range(2):
            for e in range(2):
                start_at(both(d, e), diag_copies(d, e), 0)
        for e in range(2):
            start_at(has_blk(SEC_DIRS[e]), blk_copies(e), 0)
    for d in range(2):
        start_at(has_sec(SEC_DIRS[d]), sec_copies(d), 1)
    for d in range(2):
        start_at(has_sec(SEC_DIRS[d]), sec_copies(d), 2)
    for d in range(2):
        start_at(has_sec(SEC_DIRS[d]), sec_copies(d), 3)
        for e in range(2):
            start_at(both(d, e), diag_copies(d, e), 1)
    for e in range(2):
        start_at(has_blk(SEC_DIRS[e]), blk_copies(e), 1)

    for f in range(FIELDS):
        ext[f, 0] = jnp.zeros(ext.shape[2:], jnp.float32)
        ext[f, thick + 1] = jnp.zeros(ext.shape[2:], jnp.float32)

    def make_kernel(band, widths):
        def width_at(step):
            at = lax.broadcasted_iota(jnp.int32, (1, lanes), 1) == blk + step
            total = jnp.sum(jnp.where(at, widths, 0.0), axis=1, keepdims=True)
            return jnp.maximum(total, 1.0)

        def fill(first, column, count, width):
            col = lax.broadcasted_iota(jnp.int32, (count, face_map.shape[1]), 0) + column
            distance = jnp.abs(col - face_map[...]).astype(jnp.float32)
            decay = jnp.exp(distance * (-math.pi / 2.0 / width))
            value = decay / (width + width * (decay * decay))
            high = value.astype(jnp.bfloat16)
            low = (value - high.astype(jnp.float32)).astype(jnp.bfloat16)
            k_hi[band, pl.ds(first, count), :] = high
            k_lo[band, pl.ds(first, count), :] = low

        here = width_at(0)
        chunk = 32

        def some(i, carry):
            fill(pl.multiple_of(i * chunk, chunk), blk * ocols + i * chunk, chunk, here)
            return carry

        lax.fori_loop(0, ocols // chunk, some, 0)
        blank = jnp.zeros((oext_cols - ocols - 32, face_map.shape[1]), jnp.bfloat16)
        k_hi[band, ocols + 16:oext_cols - 16, :] = blank
        k_lo[band, ocols + 16:oext_cols - 16, :] = blank
        fill(ocols, blk * ocols + ocols, 16, width_at(1))
        fill(oext_cols - 16, blk * ocols - 16, 16, width_at(-1))

    make_kernel(1, wown[0:1, :])
    for d in range(2):
        @pl.when(has_sec(-SEC_DIRS[d]))
        def _():
            sec_copies(d)[1].wait_recv()
        make_kernel(2 * d, wrecv[d, 0:1, :])

    def wait_if(condition, copy):
        @pl.when(condition)
        def _():
            copy.wait_recv()

    def assemble(t, carry):
        picks = (lane & 3) < 2
        ext_pack[t, 0:rows, :] = jnp.where(picks, recv_pack[1, t], recv_pack[0, t])
        few = picks[0:HALO]
        after, before = pl.ds(rows, HALO), pl.ds(ext_rows - HALO, HALO)
        ext_pack[t, after, :] = jnp.where(few, recv_corner[1, 1, t], recv_corner[1, 0, t])
        ext_pack[t, before, :] = jnp.where(few, recv_corner[0, 1, t], recv_corner[0, 0, t])
        sides = ext_pack[t]
        for f in range(ALL):
            ext[f, t + 1, after, 0:lanes] = recv_rows[1, t, HALO * f:HALO * f + HALO, :]
            ext[f, t + 1, before, 0:lanes] = recv_rows[0, t, HALO * f:HALO * f + HALO, :]
            ext[f, t + 1, :, lanes:2 * lanes] = (
                pltpu.roll(sides, lanes - 4 * f, 1) if f else sides)
        return carry

    def velocity_1(u, s11, s11_next, s12, s13):
        return ext[V1, u] + time_step * ext[BUO, u] * (
            (s11_next - s11) + (s12 - rows_down(s12)) + (s13 - lanes_down(s13)))

    def velocity(t, carry):
        u = t + 1
        s12, s13, s23 = ext[S12, u], ext[S13, u], ext[S23, u]
        scale = time_step * ext[BUO, u]
        s22, s33 = ext[S22, u], ext[S33, u]
        ext[V1, u] = velocity_1(u, ext[S11, u], ext[S11, u + 1], s12, s13)
        ext[V2, u] = ext[V2, u] + scale * (
            (rows_up(s22) - s22) + (s12 - ext[S12, u - 1]) + (s23 - lanes_down(s23)))
        ext[V3, u] = ext[V3, u] + scale * (
            (lanes_up(s33) - s33) + (s13 - ext[S13, u - 1]) + (s23 - rows_down(s23)))
        return carry

    def strains(u):
        v1, v2, v3 = ext[V1, u], ext[V2, u], ext[V3, u]
        return v1 - ext[V1, u - 1], v2 - rows_down(v2), v3 - lanes_down(v3)

    def stress_values(u):
        v1, v2, v3 = ext[V1, u], ext[V2, u], ext[V3, u]
        e1, e2, e3 = strains(u)
        scale = time_step * ext[MU, u]
        common = time_step * ext[LAM, u] * (e1 + e2 + e3)
        twice = 2.0 * scale
        return (
            (S11, ext[S11, u] + (common + twice * e1)),
            (S22, ext[S22, u] + (common + twice * e2)),
            (S33, ext[S33, u] + (common + twice * e3)),
            (S23, ext[S23, u] + scale * ((lanes_up(v2) - v2) + (rows_up(v3) - v3))),
            (S13, ext[S13, u] + scale * ((lanes_up(v1) - v1) + (ext[V3, u + 1] - v3))),
            (S12, ext[S12, u] + scale * ((rows_up(v1) - v1) + (ext[V2, u + 1] - v2))),
        )

    def stress(t, carry):
        for f, value in stress_values(t + 1):
            ext[f, t + 1] = value
        return carry

    def last_stress(t, carry):
        for f in (V1, V2, V3):
            slab_out[f, t] = ext[f, t + 1, 0:rows, 0:lanes]
        for f, value in stress_values(t + 1):
            slab_out[f, t] = value[0:rows, 0:lanes]
        return carry

    for d in range(2):
        wait_if(has_sec(-SEC_DIRS[d]), sec_copies(d)[0])
        for e in range(2):
            wait_if(from_both(d, e), diag_copies(d, e)[0])
    for e in range(2):
        wait_if(has_blk(-SEC_DIRS[e]), blk_copies(e)[0])
    lax.fori_loop(0, FRONT, assemble, 0)
    velocity(0, 0)
    velocity(1, 0)
    stress(0, 0)
    e1, e2, e3 = strains(2)
    s11_next = ext[S11, 2] + time_step * (
        ext[LAM, 2] * (e1 + e2 + e3) + 2.0 * ext[MU, 2] * e1)
    second = velocity_1(1, ext[S11, 1], s11_next, ext[S12, 1], ext[S13, 1])
    rise = time_step * (ext[V1, 1] + second)
    uplift[blk, OHALO:OHALO + rows, :] = rise[0:rows, 0:lanes]

    own_rows = pl.ds(OHALO, rows)

    def up_copy(d, turn):
        step = (1, -1, 0)[d]
        src = (pl.ds(OHALO + rows - OHALO, OHALO), pl.ds(OHALO, OHALO), own_rows)[d]
        dst = (pl.ds(0, OHALO), pl.ds(OHALO + rows, OHALO), own_rows)[d]
        return pltpu.make_async_remote_copy(
            src_ref=uplift.at[blk, src], dst_ref=uplift.at[blk, dst],
            send_sem=up_send.at[d, turn], recv_sem=up_recv.at[d, turn],
            device_id=(sec + step, lax.rem(blk + turn, n_blk)), device_id_type=MESH)

    def up_arrival(d, turn):
        owner = lax.rem(blk + n_blk - turn, n_blk)
        step = (1, -1, 0)[d]
        dst = (pl.ds(0, OHALO), pl.ds(OHALO + rows, OHALO), own_rows)[d]
        return pltpu.make_async_remote_copy(
            src_ref=uplift.at[owner, dst], dst_ref=uplift.at[owner, dst],
            send_sem=up_send.at[d, turn], recv_sem=up_recv.at[d, turn],
            device_id=(sec + step, lax.rem(blk + turn, n_blk)), device_id_type=MESH)

    for d in range(2):
        @pl.when(has_sec(SEC_DIRS[d]))
        def _():
            for turn in range(n_blk):
                up_copy(d, turn).start()
    for turn in range(1, n_blk):
        up_copy(2, turn).start()

    for d in range(2):
        wait_if(has_sec(-SEC_DIRS[d]), sec_copies(d)[2])
    lax.fori_loop(FRONT, thick, assemble, 0)
    lax.fori_loop(2, thick, velocity, 0)
    lax.fori_loop(1, thick, stress, 0)
    lax.fori_loop(0, thick, velocity, 0)
    lax.fori_loop(0, thick, last_stress, 0)

    for d in range(2):
        @pl.when(has_sec(-SEC_DIRS[d]))
        def _():
            sec_copies(d)[3].wait_recv()
            for turn in range(n_blk):
                up_arrival(d, turn).wait_recv()
        for e in range(2):
            wait_if(from_both(d, e), diag_copies(d, e)[1])
    for turn in range(1, n_blk):
        up_arrival(2, turn).wait_recv()
    for e in range(2):
        wait_if(has_blk(-SEC_DIRS[e]), blk_copies(e)[1])

    all_rows = rows + 2 * OHALO
    right = (lax.broadcasted_iota(jnp.int32, (rows, lanes), 1) & 15) < 8
    side_rows = jnp.concatenate([
        jnp.where(right[0:OHALO], recv_ocorner[0, 1], recv_ocorner[0, 0]),
        jnp.where(right, recv_opack[1], recv_opack[0]),
        jnp.where(right[0:OHALO], recv_ocorner[1, 1], recv_ocorner[1, 0]),
    ], axis=0)
    state = []
    for a in range(4):
        sides = pltpu.roll(side_rows, lanes - 16 * a, 1) if a else side_rows
        state.append(jnp.concatenate([oext[a, :, 0:ocols], sides], axis=1))
    surface, flux_strike, flux_dip, still = state

    whole = jnp.concatenate([uplift[b] for b in range(n_blk)], axis=1)
    high = whole.astype(jnp.bfloat16)
    low = (whole - high.astype(jnp.float32)).astype(jnp.bfloat16)
    stacked = jnp.concatenate([high, low], axis=0)

    def filtered(band):
        dims = (((1,), (1,)), ((), ()))
        first = lax.dot_general(stacked, k_hi[band], dims, preferred_element_type=jnp.float32)
        second = lax.dot_general(high, k_lo[band], dims, preferred_element_type=jnp.float32)
        return first[0:all_rows] + (first[all_rows:] + second)

    source = jnp.concatenate([
        filtered(0)[0:OHALO], filtered(1)[OHALO:OHALO + rows], filtered(2)[OHALO + rows:]], axis=0)

    row_at = lax.broadcasted_iota(jnp.int32, (all_rows, oext_cols), 0) + (sec * rows - OHALO)
    col = lax.broadcasted_iota(jnp.int32, (all_rows, oext_cols), 1)
    col_at = jnp.where(col < ocols + lanes // 2, col, col - oext_cols) + blk * ocols
    wet = ((row_at >= 0) & (row_at < n_sec * rows)) & ((col_at >= 0) & (col_at < n_blk * ocols))
    surface = jnp.where(wet, surface + source, 0.0)
    pull = wave_step * 0.5 * still
    for _ in range(WAVE_STEPS):
        change = (rows_up(flux_strike) - rows_down(flux_strike)) + (
            lanes_up(flux_dip) - lanes_down(flux_dip))
        surface = jnp.where(wet, surface - wave_step * 0.5 * change, 0.0)
        flux_strike = flux_strike - pull * (rows_up(surface) - rows_down(surface))
        flux_dip = flux_dip - pull * (lanes_up(surface) - lanes_down(surface))
    for a, value in enumerate((surface, flux_strike, flux_dip)):
        ocean_out[a] = value[OHALO:OHALO + rows, 0:ocols]

    for d in range(2):
        @pl.when(has_sec(SEC_DIRS[d]))
        def _():
            for copy in sec_copies(d):
                copy.wait_send()
            for turn in range(n_blk):
                up_copy(d, turn).wait_send()
        for e in range(2):
            @pl.when(both(d, e))
            def _():
                for copy in diag_copies(d, e):
                    copy.wait_send()
    for e in range(2):
        @pl.when(has_blk(SEC_DIRS[e]))
        def _():
            for copy in blk_copies(e):
                copy.wait_send()
    for turn in range(1, n_blk):
        up_copy(2, turn).wait_send()


def on_device(
    slab_state, buoyancy, lame_lambda, lame_mu, face_map, band_widths, ocean_state, water_depth
):
    n_blk = lax.axis_size("blk")
    thick, rows, lanes = slab_state.shape[1:]
    ocols = ocean_state.shape[2]
    dip = face_map.shape[0]
    ext_rows = rows + 8
    oext_cols = ocols + lanes
    f32 = jnp.float32
    vmem = pl.BlockSpec(memory_space=pltpu.VMEM)
    dma = pltpu.SemaphoreType.DMA
    return pl.pallas_call(
        kernel_body,
        out_shape=(
            jax.ShapeDtypeStruct(slab_state.shape, f32),
            jax.ShapeDtypeStruct(ocean_state.shape, f32),
        ),
        in_specs=[vmem] * 8,
        out_specs=(vmem, vmem),
        scratch_shapes=[
            pltpu.VMEM((ALL, thick + 2, ext_rows, 2 * lanes), f32),
            pltpu.VMEM((2, thick, ALL * HALO, lanes), f32),
            pltpu.VMEM((2, thick, ALL * HALO, lanes), f32),
            pltpu.VMEM((thick, rows, lanes), f32),
            pltpu.VMEM((2, thick, rows, lanes), f32),
            pltpu.VMEM((2, thick, HALO, lanes), f32),
            pltpu.VMEM((2, 2, thick, HALO, lanes), f32),
            pltpu.VMEM((thick, ext_rows, lanes), f32),
            pltpu.VMEM((4, rows + 2 * OHALO, oext_cols), f32),
            pltpu.VMEM((rows, lanes), f32),
            pltpu.VMEM((2, rows, lanes), f32),
            pltpu.VMEM((2, 2, OHALO, lanes), f32),
            pltpu.VMEM((8, lanes), f32),
            pltpu.VMEM((2, 8, lanes), f32),
            pltpu.VMEM((n_blk, rows + 2 * OHALO, lanes), f32),
            pltpu.VMEM((3, oext_cols, dip), jnp.bfloat16),
            pltpu.VMEM((3, oext_cols, dip), jnp.bfloat16),
            dma((2, 4)), dma((2, 4)),
            dma((2, 2)), dma((2, 2)),
            dma((2, 2, 2)), dma((2, 2, 2)),
            dma((3, n_blk)), dma((3, n_blk)),
        ],
        compiler_params=pltpu.CompilerParams(
            collective_id=0, has_side_effects=True, vmem_limit_bytes=40 * 1024 * 1024
        ),
        cost_estimate=pl.CostEstimate(
            flops=200_000_000, bytes_accessed=2_000_000, transcendentals=500_000),
    )(
        slab_state, buoyancy, lame_lambda, lame_mu, face_map.reshape(1, dip), band_widths,
        ocean_state, water_depth,
    )


def solution(mesh):
    in_specs = (
        P(None, None, "sec", "blk"),
        P(None, "sec", "blk"),
        P(None, "sec", "blk"),
        P(None, "sec", "blk"),
        P(),
        P("sec", None),
        P(None, "sec", "blk"),
        P("sec", "blk"),
    )
    out_specs = (P(None, None, "sec", "blk"), P(None, "sec", "blk"))
    return jax.shard_map(
        on_device, mesh=mesh, in_specs=in_specs, out_specs=out_specs, check_vma=False
    )
```

```python
import functools
import math

import jax
import jax.numpy as jnp
from jax import lax
from jax.experimental import pallas as pl
from jax.experimental.pallas import tpu as pltpu
from jax.sharding import PartitionSpec as P

MESH = pl.DeviceIdType.MESH
WAVE_STEPS = 4
time_step = 0.25
wave_step = 0.5

V1, V2, V3, S11, S22, S33, S23, S13, S12, BUO, LAM, MU = range(12)
FIELDS = 9
ALL = 12
HALO = 2
OHALO = 8
FRONT = 3

SEC_DIRS = (1, -1)


def rows_up(x):
    return pltpu.roll(x, x.shape[0] - 1, 0)


def rows_down(x):
    return pltpu.roll(x, 1, 0)


def lanes_up(x):
    return pltpu.roll(x, x.shape[1] - 1, 1)


def lanes_down(x):
    return pltpu.roll(x, 1, 1)


def kernel_body(
    slab, buoyancy, lame_lambda, lame_mu, face_hbm, bands_hbm, ocean, depth,
    slab_out, ocean_out,
    ext, send_rows, recv_rows, pack, recv_pack, send_corner, recv_corner, ext_pack,
    oext, opack, recv_opack, recv_ocorner, face_map, bands, uplift, source, k_hi, k_lo,
    load_sem, sec_send, sec_recv, blk_send, blk_recv, diag_send, diag_recv,
    up_send, up_recv, src_send, src_recv,
):
    n_sec = lax.axis_size("sec")
    n_blk = lax.axis_size("blk")
    sec = lax.axis_index("sec")
    blk = lax.axis_index("blk")
    thick, rows, lanes = slab.shape[1:]
    ext_rows = ext.shape[2]
    ocols = ocean.shape[2]
    oext_cols = oext.shape[2]
    dip = face_map.shape[1]
    tile_cols = bands.shape[1]
    front, back = pl.ds(0, FRONT), pl.ds(FRONT, thick - FRONT)

    def has_sec(step):
        return sec + step < n_sec if step > 0 else sec + step >= 0

    def has_blk(step):
        return blk + step < n_blk if step > 0 else blk + step >= 0

    own_rows, own_lanes = pl.ds(0, rows), pl.ds(0, lanes)
    ocean_rows, ocean_cols = pl.ds(OHALO, rows), pl.ds(0, ocols)
    layers = pl.ds(1, thick)
    loads = [
        (slab, ext.at[pl.ds(0, FIELDS), layers, own_rows, own_lanes]),
        (buoyancy, ext.at[BUO, layers, own_rows, own_lanes]),
        (lame_lambda, ext.at[LAM, layers, own_rows, own_lanes]),
        (lame_mu, ext.at[MU, layers, own_rows, own_lanes]),
        (face_hbm, face_map),
        (bands_hbm, bands),
        (ocean, oext.at[pl.ds(0, 3), ocean_rows, ocean_cols]),
        (depth, oext.at[3, ocean_rows, ocean_cols]),
    ]
    loads = [pltpu.make_async_copy(src, dst, load_sem.at[i]) for i, (src, dst) in enumerate(loads)]
    for load in loads:
        load.start()

    recv_rows[...] = jnp.zeros_like(recv_rows)
    recv_pack[...] = jnp.zeros_like(recv_pack)
    recv_corner[...] = jnp.zeros_like(recv_corner)
    recv_opack[...] = jnp.zeros_like(recv_opack)
    recv_ocorner[...] = jnp.zeros_like(recv_ocorner)
    for first in (0, OHALO + rows):
        source[first:first + OHALO, :] = jnp.zeros((OHALO, oext_cols), jnp.float32)
        oext[:, first:first + OHALO, 0:ocols] = jnp.zeros((4, OHALO, ocols), jnp.float32)

    barrier = pltpu.get_barrier_semaphore()

    def greet(step, turn):
        pl.semaphore_signal(
            barrier, inc=1,
            device_id=(sec + step, lax.rem(blk + turn, n_blk)), device_id_type=MESH,
        )

    for turn in range(1, n_blk):
        greet(0, turn)
    for step in SEC_DIRS:
        @pl.when(has_sec(step))
        def _():
            for turn in range(n_blk):
                greet(step, turn)

    for f in range(FIELDS):
        ext[f, 0] = jnp.zeros(ext.shape[2:], jnp.float32)
        ext[f, thick + 1] = jnp.zeros(ext.shape[2:], jnp.float32)

    def remote(src, dst, send_sem, recv_sem, target):
        return pltpu.make_async_remote_copy(
            src_ref=src, dst_ref=dst, send_sem=send_sem, recv_sem=recv_sem,
            device_id=target, device_id_type=MESH)

    def sec_copy(d, i):
        out_rows = pl.ds(rows, OHALO) if d == 0 else pl.ds(OHALO, OHALO)
        to_rows = pl.ds(0, OHALO) if d == 0 else pl.ds(OHALO + rows, OHALO)
        if i == 2:
            src, dst = oext.at[:, out_rows, ocean_cols], oext.at[:, to_rows, ocean_cols]
        else:
            part = (front, back)[i]
            src, dst = send_rows.at[d, part], recv_rows.at[d, part]
        return remote(src, dst, sec_send.at[d, i], sec_recv.at[d, i], (sec + SEC_DIRS[d], blk))

    def blk_copy(e, i):
        if i == 2:
            src, dst = opack, recv_opack.at[e]
        else:
            part = (front, back)[i]
            src, dst = pack.at[part], recv_pack.at[e, part]
        return remote(src, dst, blk_send.at[e, i], blk_recv.at[e, i], (sec, blk + SEC_DIRS[e]))

    def diag_copy(d, e, i):
        if i == 2:
            src = opack.at[pl.ds(rows - OHALO, OHALO) if d == 0 else pl.ds(0, OHALO)]
            dst = recv_ocorner.at[d, e]
        else:
            part = (front, back)[i]
            src, dst = send_corner.at[d, part], recv_corner.at[d, e, part]
        return remote(src, dst, diag_send.at[d, e, i], diag_recv.at[d, e, i],
                      (sec + SEC_DIRS[d], blk + SEC_DIRS[e]))

    def both(d, e):
        return jnp.logical_and(has_sec(SEC_DIRS[d]), has_blk(SEC_DIRS[e]))

    def from_both(d, e):
        return jnp.logical_and(has_sec(-SEC_DIRS[d]), has_blk(-SEC_DIRS[e]))

    def send_all(i):
        for d in range(2):
            @pl.when(has_sec(SEC_DIRS[d]))
            def _():
                sec_copy(d, i).start()
        for d in range(2):
            for e in range(2):
                @pl.when(both(d, e))
                def _():
                    diag_copy(d, e, i).start()
        for e in range(2):
            @pl.when(has_blk(SEC_DIRS[e]))
            def _():
                blk_copy(e, i).start()

    def await_all(i):
        for d in range(2):
            @pl.when(has_sec(-SEC_DIRS[d]))
            def _():
                sec_copy(d, i).wait_recv()
            for e in range(2):
                @pl.when(from_both(d, e))
                def _():
                    diag_copy(d, e, i).wait_recv()
        for e in range(2):
            @pl.when(has_blk(-SEC_DIRS[e]))
            def _():
                blk_copy(e, i).wait_recv()

    lane = lax.broadcasted_iota(jnp.int32, (rows, lanes), 1)

    def pack_layer(t):
        packed = jnp.zeros((rows, lanes), jnp.float32)
        for f in range(ALL):
            value = ext[f, t + 1, 0:rows, 0:lanes]
            send_rows[0, t, HALO * f:HALO * f + HALO, :] = value[rows - HALO:, :]
            send_rows[1, t, HALO * f:HALO * f + HALO, :] = value[0:HALO, :]
            moved = pltpu.roll(value, 4 * f, 1) if f else value
            packed = jnp.where(((lane - 4 * f + 2) & (lanes - 1)) < 4, moved, packed)
        pack[t] = packed
        send_corner[0, t] = packed[rows - HALO:, :]
        send_corner[1, t] = packed[0:HALO, :]

    for load in loads[:4]:
        load.wait()
    for t in range(FRONT):
        pack_layer(t)
    near = (n_blk - 1) + sum(jnp.where(has_sec(step), n_blk, 0) for step in SEC_DIRS)
    pl.semaphore_wait(barrier, near)
    send_all(0)
    for t in range(FRONT, thick):
        pack_layer(t)
    send_all(1)

    for load in loads[4:]:
        load.wait()
    opacked = jnp.zeros((rows, lanes), jnp.float32)
    for a in range(4):
        value = oext[a, OHALO:OHALO + rows, 0:ocols]
        edges = jnp.where(lane < lanes // 2, value[:, 0:lanes], value[:, ocols - lanes:])
        moved = pltpu.roll(edges, 16 * a, 1) if a else edges
        opacked = jnp.where(((lane - 16 * a + 8) & (lanes - 1)) < 16, moved, opacked)
    opack[...] = opacked
    send_all(2)

    def width_at(step):
        total = jnp.zeros((1, 1), jnp.float32)
        for j in range(tile_cols):
            total = jnp.where(blk + step == j, bands[0:1, j:j + 1].astype(jnp.float32), total)
        return jnp.maximum(total, 1.0)

    chunk = 32
    face = face_map[...].astype(jnp.float32)
    index = lax.broadcasted_iota(jnp.int32, (chunk, dip), 0).astype(jnp.float32)
    own_column = (blk * ocols).astype(jnp.float32)

    def fill(first, column, count, width):
        distance = jnp.abs((index[0:count] + (own_column + float(column))) - face)
        decay = jnp.exp2(distance * (-math.pi / 2.0 * math.log2(math.e) / width))
        under = width + width * (decay * decay)
        guess = pl.reciprocal(under, approx=True)
        value = decay * (guess * (2.0 - under * guess))
        high = value.astype(jnp.bfloat16)
        k_hi[first:first + count, :] = high
        k_lo[first:first + count, :] = (value - high.astype(jnp.float32)).astype(jnp.bfloat16)

    here = width_at(0)
    for first in range(0, ocols, chunk):
        fill(first, first, chunk, here)
    fill(ocols, ocols, 16, width_at(1))
    fill(oext_cols - 16, -16, 16, width_at(-1))
    blank = jnp.zeros((oext_cols - ocols - 32, dip), jnp.bfloat16)
    k_hi[ocols + 16:oext_cols - 16, :] = blank
    k_lo[ocols + 16:oext_cols - 16, :] = blank

    picks = (lane & 3) < 2

    def assemble(t):
        ext_pack[t, 0:rows, :] = jnp.where(picks, recv_pack[1, t], recv_pack[0, t])
        few = picks[0:HALO]
        after, before = pl.ds(rows, HALO), pl.ds(ext_rows - HALO, HALO)
        ext_pack[t, after, :] = jnp.where(few, recv_corner[1, 1, t], recv_corner[1, 0, t])
        ext_pack[t, before, :] = jnp.where(few, recv_corner[0, 1, t], recv_corner[0, 0, t])
        sides = ext_pack[t]
        for f in range(ALL):
            ext[f, t + 1, after, 0:lanes] = recv_rows[1, t, HALO * f:HALO * f + HALO, :]
            ext[f, t + 1, before, 0:lanes] = recv_rows[0, t, HALO * f:HALO * f + HALO, :]
            ext[f, t + 1, :, lanes:2 * lanes] = (
                pltpu.roll(sides, lanes - 4 * f, 1) if f else sides)

    def velocity_1(u, s11, s11_next, s12, s13):
        return ext[V1, u] + time_step * ext[BUO, u] * (
            (s11_next - s11) + (s12 - rows_down(s12)) + (s13 - lanes_down(s13)))

    def velocity(t):
        u = t + 1
        s12, s13, s23 = ext[S12, u], ext[S13, u], ext[S23, u]
        scale = time_step * ext[BUO, u]
        s22, s33 = ext[S22, u], ext[S33, u]
        ext[V1, u] = velocity_1(u, ext[S11, u], ext[S11, u + 1], s12, s13)
        ext[V2, u] = ext[V2, u] + scale * (
            (rows_up(s22) - s22) + (s12 - ext[S12, u - 1]) + (s23 - lanes_down(s23)))
        ext[V3, u] = ext[V3, u] + scale * (
            (lanes_up(s33) - s33) + (s13 - ext[S13, u - 1]) + (s23 - rows_down(s23)))

    def strains(u):
        v1, v2, v3 = ext[V1, u], ext[V2, u], ext[V3, u]
        return v1 - ext[V1, u - 1], v2 - rows_down(v2), v3 - lanes_down(v3)

    def stress_values(u):
        v1, v2, v3 = ext[V1, u], ext[V2, u], ext[V3, u]
        e1, e2, e3 = strains(u)
        scale = time_step * ext[MU, u]
        common = time_step * ext[LAM, u] * (e1 + e2 + e3)
        twice = 2.0 * scale
        return (
            (S11, ext[S11, u] + (common + twice * e1)),
            (S22, ext[S22, u] + (common + twice * e2)),
            (S33, ext[S33, u] + (common + twice * e3)),
            (S23, ext[S23, u] + scale * ((lanes_up(v2) - v2) + (rows_up(v3) - v3))),
            (S13, ext[S13, u] + scale * ((lanes_up(v1) - v1) + (ext[V3, u + 1] - v3))),
            (S12, ext[S12, u] + scale * ((rows_up(v1) - v1) + (ext[V2, u + 1] - v2))),
        )

    def stress(t):
        for f, value in stress_values(t + 1):
            ext[f, t + 1] = value

    def last_stress(t):
        for f in (V1, V2, V3):
            slab_out[f, t] = ext[f, t + 1, 0:rows, 0:lanes]
        for f, value in stress_values(t + 1):
            slab_out[f, t] = value[0:rows, 0:lanes]

    await_all(0)
    for t in range(FRONT):
        assemble(t)
    velocity(0)
    velocity(1)
    stress(0)
    e1, e2, e3 = strains(2)
    s11_next = ext[S11, 2] + time_step * (
        ext[LAM, 2] * (e1 + e2 + e3) + 2.0 * ext[MU, 2] * e1)
    second = velocity_1(1, ext[S11, 1], s11_next, ext[S12, 1], ext[S13, 1])
    rise = time_step * (ext[V1, 1] + second)
    uplift[blk] = rise[0:rows, 0:lanes]

    def up_copy(turn):
        return remote(uplift.at[blk], uplift.at[blk], up_send.at[turn], up_recv.at[turn],
                      (sec, lax.rem(blk + turn, n_blk)))

    def up_arrival(turn):
        owner = lax.rem(blk + n_blk - turn, n_blk)
        return remote(uplift.at[owner], uplift.at[owner], up_send.at[turn], up_recv.at[turn],
                      (sec, lax.rem(blk + turn, n_blk)))

    for turn in range(1, n_blk):
        up_copy(turn).start()

    await_all(1)
    for t in range(FRONT, thick):
        assemble(t)
    for t in range(2, thick):
        velocity(t)
    for t in range(1, thick):
        stress(t)

    for turn in range(1, n_blk):
        up_arrival(turn).wait_recv()
    whole = jnp.concatenate([uplift[b] for b in range(n_blk)], axis=1)
    high = whole.astype(jnp.bfloat16)
    low = (whole - high.astype(jnp.float32)).astype(jnp.bfloat16)
    dims = (((1,), (1,)), ((), ()))
    by_high = lax.dot_general(jnp.concatenate([high, low], axis=0), k_hi[...], dims,
                              preferred_element_type=jnp.float32)
    by_low = lax.dot_general(high, k_lo[...], dims, preferred_element_type=jnp.float32)
    source[OHALO:OHALO + rows, :] = by_high[0:rows] + (by_high[rows:] + by_low)

    def src_copy(d):
        out_rows = pl.ds(rows, OHALO) if d == 0 else pl.ds(OHALO, OHALO)
        to_rows = pl.ds(0, OHALO) if d == 0 else pl.ds(OHALO + rows, OHALO)
        return remote(source.at[out_rows], source.at[to_rows], src_send.at[d], src_recv.at[d],
                      (sec + SEC_DIRS[d], blk))

    for d in range(2):
        @pl.when(has_sec(SEC_DIRS[d]))
        def _():
            src_copy(d).start()

    for t in range(thick):
        velocity(t)
    for t in range(thick):
        last_stress(t)

    await_all(2)
    for d in range(2):
        @pl.when(has_sec(-SEC_DIRS[d]))
        def _():
            src_copy(d).wait_recv()

    all_rows = rows + 2 * OHALO
    right = (lane & 15) < 8
    side_rows = jnp.concatenate([
        jnp.where(right[0:OHALO], recv_ocorner[0, 1], recv_ocorner[0, 0]),
        jnp.where(right, recv_opack[1], recv_opack[0]),
        jnp.where(right[0:OHALO], recv_ocorner[1, 1], recv_ocorner[1, 0]),
    ], axis=0)
    state = []
    for a in range(4):
        sides = pltpu.roll(side_rows, lanes - 16 * a, 1) if a else side_rows
        state.append(jnp.concatenate([oext[a, :, 0:ocols], sides], axis=1))
    surface, flux_strike, flux_dip, still = state

    row_at = lax.broadcasted_iota(jnp.int32, (all_rows, oext_cols), 0) + (sec * rows - OHALO)
    col = lax.broadcasted_iota(jnp.int32, (all_rows, oext_cols), 1)
    col_at = jnp.where(col < ocols + lanes // 2, col, col - oext_cols) + blk * ocols
    wet = ((row_at >= 0) & (row_at < n_sec * rows)) & ((col_at >= 0) & (col_at < n_blk * ocols))
    surface = jnp.where(wet, surface + source[...], 0.0)
    pull = wave_step * 0.5 * still
    for _ in range(WAVE_STEPS):
        change = (rows_up(flux_strike) - rows_down(flux_strike)) + (
            lanes_up(flux_dip) - lanes_down(flux_dip))
        surface = jnp.where(wet, surface - wave_step * 0.5 * change, 0.0)
        flux_strike = flux_strike - pull * (rows_up(surface) - rows_down(surface))
        flux_dip = flux_dip - pull * (lanes_up(surface) - lanes_down(surface))
    for a, value in enumerate((surface, flux_strike, flux_dip)):
        ocean_out[a] = value[OHALO:OHALO + rows, 0:ocols]

    for d in range(2):
        @pl.when(has_sec(SEC_DIRS[d]))
        def _():
            for i in range(3):
                sec_copy(d, i).wait_send()
            src_copy(d).wait_send()
        for e in range(2):
            @pl.when(both(d, e))
            def _():
                for i in range(3):
                    diag_copy(d, e, i).wait_send()
    for e in range(2):
        @pl.when(has_blk(SEC_DIRS[e]))
        def _():
            for i in range(3):
                blk_copy(e, i).wait_send()
    for turn in range(1, n_blk):
        up_copy(turn).wait_send()


def on_device(
    slab_state, buoyancy, lame_lambda, lame_mu, face_map, band_widths, ocean_state, water_depth
):
    n_blk = lax.axis_size("blk")
    thick, rows, lanes = slab_state.shape[1:]
    ocols = ocean_state.shape[2]
    dip = face_map.shape[0]
    ext_rows = rows + 8
    oext_cols = ocols + lanes
    f32 = jnp.float32
    vmem = pl.BlockSpec(memory_space=pltpu.VMEM)
    hbm = pl.BlockSpec(memory_space=pltpu.HBM)
    dma = pltpu.SemaphoreType.DMA
    return pl.pallas_call(
        kernel_body,
        out_shape=(
            jax.ShapeDtypeStruct(slab_state.shape, f32),
            jax.ShapeDtypeStruct(ocean_state.shape, f32),
        ),
        in_specs=[hbm] * 8,
        out_specs=(vmem, vmem),
        scratch_shapes=[
            pltpu.VMEM((ALL, thick + 2, ext_rows, 2 * lanes), f32),
            pltpu.VMEM((2, thick, ALL * HALO, lanes), f32),
            pltpu.VMEM((2, thick, ALL * HALO, lanes), f32),
            pltpu.VMEM((thick, rows, lanes), f32),
            pltpu.VMEM((2, thick, rows, lanes), f32),
            pltpu.VMEM((2, thick, HALO, lanes), f32),
            pltpu.VMEM((2, 2, thick, HALO, lanes), f32),
            pltpu.VMEM((thick, ext_rows, lanes), f32),
            pltpu.VMEM((4, rows + 2 * OHALO, oext_cols), f32),
            pltpu.VMEM((rows, lanes), f32),
            pltpu.VMEM((2, rows, lanes), f32),
            pltpu.VMEM((2, 2, OHALO, lanes), f32),
            pltpu.VMEM((1, dip), jnp.int32),
            pltpu.VMEM(band_widths.shape, jnp.int32),
            pltpu.VMEM((n_blk, rows, lanes), f32),
            pltpu.VMEM((rows + 2 * OHALO, oext_cols), f32),
            pltpu.VMEM((oext_cols, dip), jnp.bfloat16),
            pltpu.VMEM((oext_cols, dip), jnp.bfloat16),
            dma((8,)),
            dma((2, 3)), dma((2, 3)),
            dma((2, 3)), dma((2, 3)),
            dma((2, 2, 3)), dma((2, 2, 3)),
            dma((n_blk,)), dma((n_blk,)),
            dma((2,)), dma((2,)),
        ],
        compiler_params=pltpu.CompilerParams(
            collective_id=0, has_side_effects=True, vmem_limit_bytes=62 * 1024 * 1024
        ),
        cost_estimate=pl.CostEstimate(
            flops=200_000_000, bytes_accessed=2_000_000, transcendentals=500_000),
    )(
        slab_state, buoyancy, lame_lambda, lame_mu, face_map.reshape(1, dip), band_widths,
        ocean_state, water_depth,
    )


def solution(mesh):
    in_specs = (
        P(None, None, "sec", "blk"),
        P(None, "sec", "blk"),
        P(None, "sec", "blk"),
        P(None, "sec", "blk"),
        P(),
        P("sec", None),
        P(None, "sec", "blk"),
        P("sec", "blk"),
    )
    out_specs = (P(None, None, "sec", "blk"), P(None, "sec", "blk"))
    return jax.shard_map(
        on_device, mesh=mesh, in_specs=in_specs, out_specs=out_specs, check_vma=False
    )
```

```python
import functools
import math

import jax
import jax.numpy as jnp
from jax import lax
from jax.experimental import pallas as pl
from jax.experimental.pallas import tpu as pltpu
from jax.sharding import PartitionSpec as P

MESH = pl.DeviceIdType.MESH
WAVE_STEPS = 4
time_step = 0.25
wave_step = 0.5

V1, V2, V3, S11, S22, S33, S23, S13, S12, BUO, LAM, MU = range(12)
FIELDS = 9
ALL = 12
HALO = 2
OHALO = 8
FRONT = 3

TWO_ROWS = ((S12, S22, S23, V2, BUO), (S11, S12, S13, S22, S23, S33, V1, V3, BUO))
ONE_ROW = ((S11, S13, S33, V1, V3, LAM, MU), (V2, LAM, MU))


def per_layer(d):
    return HALO * len(TWO_ROWS[d]) + len(ONE_ROW[d])


def part_rows(d, layers):
    return -(-per_layer(d) * layers // 8) * 8


def row_pieces(d, t):
    at = (t if t < FRONT else t - FRONT) * per_layer(d)
    for f in TWO_ROWS[d]:
        yield f, HALO, at
        at += HALO
    for f in ONE_ROW[d]:
        yield f, 1, at
        at += 1

SEC_DIRS = (1, -1)


def rows_up(x):
    return pltpu.roll(x, x.shape[0] - 1, 0)


def rows_down(x):
    return pltpu.roll(x, 1, 0)


def lanes_up(x):
    return pltpu.roll(x, x.shape[1] - 1, 1)


def lanes_down(x):
    return pltpu.roll(x, 1, 1)


def kernel_body(
    slab, buoyancy, lame_lambda, lame_mu, face_hbm, bands_hbm, ocean, depth,
    slab_out, ocean_out,
    ext, send_rows, recv_rows, pack, recv_pack, send_corner, recv_corner, ext_pack,
    oext, opack, recv_opack, recv_ocorner, face_map, bands, uplift, source, k_hi, k_lo,
    load_sem, sec_send, sec_recv, blk_send, blk_recv, diag_send, diag_recv,
    up_send, up_recv, src_send, src_recv,
):
    n_sec = lax.axis_size("sec")
    n_blk = lax.axis_size("blk")
    sec = lax.axis_index("sec")
    blk = lax.axis_index("blk")
    thick, rows, lanes = slab.shape[1:]
    ext_rows = ext.shape[2]
    ocols = ocean.shape[2]
    oext_cols = oext.shape[2]
    dip = face_map.shape[1]
    tile_cols = bands.shape[1]
    front, back = pl.ds(0, FRONT), pl.ds(FRONT, thick - FRONT)

    def has_sec(step):
        return sec + step < n_sec if step > 0 else sec + step >= 0

    def has_blk(step):
        return blk + step < n_blk if step > 0 else blk + step >= 0

    own_rows, own_lanes = pl.ds(0, rows), pl.ds(0, lanes)
    ocean_rows, ocean_cols = pl.ds(OHALO, rows), pl.ds(0, ocols)
    layers = pl.ds(1, thick)
    loads = [
        (slab, ext.at[pl.ds(0, FIELDS), layers, own_rows, own_lanes]),
        (buoyancy, ext.at[BUO, layers, own_rows, own_lanes]),
        (lame_lambda, ext.at[LAM, layers, own_rows, own_lanes]),
        (lame_mu, ext.at[MU, layers, own_rows, own_lanes]),
        (face_hbm, face_map),
        (bands_hbm, bands),
        (ocean, oext.at[pl.ds(0, 3), ocean_rows, ocean_cols]),
        (depth, oext.at[3, ocean_rows, ocean_cols]),
    ]
    loads = [pltpu.make_async_copy(src, dst, load_sem.at[i]) for i, (src, dst) in enumerate(loads)]
    for load in loads:
        load.start()

    recv_rows[...] = jnp.zeros_like(recv_rows)
    recv_pack[...] = jnp.zeros_like(recv_pack)
    recv_corner[...] = jnp.zeros_like(recv_corner)
    recv_opack[...] = jnp.zeros_like(recv_opack)
    recv_ocorner[...] = jnp.zeros_like(recv_ocorner)
    for first in (0, OHALO + rows):
        source[first:first + OHALO, :] = jnp.zeros((OHALO, oext_cols), jnp.float32)
        oext[:, first:first + OHALO, 0:ocols] = jnp.zeros((4, OHALO, ocols), jnp.float32)

    barrier = pltpu.get_barrier_semaphore()

    def greet(step, turn):
        pl.semaphore_signal(
            barrier, inc=1,
            device_id=(sec + step, lax.rem(blk + turn, n_blk)), device_id_type=MESH,
        )

    for turn in range(1, n_blk):
        greet(0, turn)
    for step in SEC_DIRS:
        @pl.when(has_sec(step))
        def _():
            for turn in range(n_blk):
                greet(step, turn)

    for f in range(FIELDS):
        ext[f, 0] = jnp.zeros(ext.shape[2:], jnp.float32)
        ext[f, thick + 1] = jnp.zeros(ext.shape[2:], jnp.float32)

    def remote(src, dst, send_sem, recv_sem, target):
        return pltpu.make_async_remote_copy(
            src_ref=src, dst_ref=dst, send_sem=send_sem, recv_sem=recv_sem,
            device_id=target, device_id_type=MESH)

    def sec_copy(d, i):
        out_rows = pl.ds(rows, OHALO) if d == 0 else pl.ds(OHALO, OHALO)
        to_rows = pl.ds(0, OHALO) if d == 0 else pl.ds(OHALO + rows, OHALO)
        if i == 2:
            src, dst = oext.at[:, out_rows, ocean_cols], oext.at[:, to_rows, ocean_cols]
        else:
            part = pl.ds(0, part_rows(d, (FRONT, thick - FRONT)[i]))
            src, dst = send_rows.at[d, i, part], recv_rows.at[d, i, part]
        return remote(src, dst, sec_send.at[d, i], sec_recv.at[d, i], (sec + SEC_DIRS[d], blk))

    def blk_copy(e, i):
        if i == 2:
            src, dst = opack, recv_opack.at[e]
        else:
            part = (front, back)[i]
            src, dst = pack.at[part], recv_pack.at[e, part]
        return remote(src, dst, blk_send.at[e, i], blk_recv.at[e, i], (sec, blk + SEC_DIRS[e]))

    def diag_copy(d, e, i):
        if i == 2:
            src = opack.at[pl.ds(rows - OHALO, OHALO) if d == 0 else pl.ds(0, OHALO)]
            dst = recv_ocorner.at[d, e]
        else:
            part = (front, back)[i]
            src, dst = send_corner.at[d, part], recv_corner.at[d, e, part]
        return remote(src, dst, diag_send.at[d, e, i], diag_recv.at[d, e, i],
                      (sec + SEC_DIRS[d], blk + SEC_DIRS[e]))

    def both(d, e):
        return jnp.logical_and(has_sec(SEC_DIRS[d]), has_blk(SEC_DIRS[e]))

    def from_both(d, e):
        return jnp.logical_and(has_sec(-SEC_DIRS[d]), has_blk(-SEC_DIRS[e]))

    def send_all(i):
        for d in range(2):
            @pl.when(has_sec(SEC_DIRS[d]))
            def _():
                sec_copy(d, i).start()
        for d in range(2):
            for e in range(2):
                @pl.when(both(d, e))
                def _():
                    diag_copy(d, e, i).start()
        for e in range(2):
            @pl.when(has_blk(SEC_DIRS[e]))
            def _():
                blk_copy(e, i).start()

    def await_all(i):
        for d in range(2):
            @pl.when(has_sec(-SEC_DIRS[d]))
            def _():
                sec_copy(d, i).wait_recv()
            for e in range(2):
                @pl.when(from_both(d, e))
                def _():
                    diag_copy(d, e, i).wait_recv()
        for e in range(2):
            @pl.when(has_blk(-SEC_DIRS[e]))
            def _():
                blk_copy(e, i).wait_recv()

    lane = lax.broadcasted_iota(jnp.int32, (rows, lanes), 1)

    def pack_layer(t):
        packed = jnp.zeros((rows, lanes), jnp.float32)
        for f in range(ALL):
            value = ext[f, t + 1, 0:rows, 0:lanes]
            moved = pltpu.roll(value, 4 * f, 1) if f else value
            packed = jnp.where(((lane - 4 * f + 2) & (lanes - 1)) < 4, moved, packed)
        i = 0 if t < FRONT else 1
        for f, count, at in row_pieces(0, t):
            send_rows[0, i, at:at + count, :] = ext[f, t + 1, rows - count:rows, 0:lanes]
        for f, count, at in row_pieces(1, t):
            send_rows[1, i, at:at + count, :] = ext[f, t + 1, 0:count, 0:lanes]
        pack[t] = packed
        send_corner[0, t] = packed[rows - HALO:, :]
        send_corner[1, t] = packed[0:HALO, :]

    for load in loads[:4]:
        load.wait()
    for t in range(FRONT):
        pack_layer(t)
    near = (n_blk - 1) + sum(jnp.where(has_sec(step), n_blk, 0) for step in SEC_DIRS)
    pl.semaphore_wait(barrier, near)
    send_all(0)
    for t in range(FRONT, thick):
        pack_layer(t)
    send_all(1)

    for load in loads[4:]:
        load.wait()
    opacked = jnp.zeros((rows, lanes), jnp.float32)
    for a in range(4):
        value = oext[a, OHALO:OHALO + rows, 0:ocols]
        edges = jnp.where(lane < lanes // 2, value[:, 0:lanes], value[:, ocols - lanes:])
        moved = pltpu.roll(edges, 16 * a, 1) if a else edges
        opacked = jnp.where(((lane - 16 * a + 8) & (lanes - 1)) < 16, moved, opacked)
    opack[...] = opacked
    send_all(2)

    def width_at(step):
        total = jnp.zeros((1, 1), jnp.float32)
        for j in range(tile_cols):
            total = jnp.where(blk + step == j, bands[0:1, j:j + 1].astype(jnp.float32), total)
        return jnp.maximum(total, 1.0)

    chunk = 32
    face = face_map[...].astype(jnp.float32)
    index = lax.broadcasted_iota(jnp.int32, (chunk, dip), 0).astype(jnp.float32)
    own_column = (blk * ocols).astype(jnp.float32)

    def fill(first, column, count, width):
        distance = jnp.abs((index[0:count] + (own_column + float(column))) - face)
        decay = jnp.exp2(distance * (-math.pi / 2.0 * math.log2(math.e) / width))
        under = width + width * (decay * decay)
        guess = pl.reciprocal(under, approx=True)
        value = decay * (guess * (2.0 - under * guess))
        high = value.astype(jnp.bfloat16)
        k_hi[first:first + count, :] = high
        k_lo[first:first + count, :] = (value - high.astype(jnp.float32)).astype(jnp.bfloat16)

    here = width_at(0)
    for first in range(0, ocols, chunk):
        fill(first, first, chunk, here)
    fill(ocols, ocols, 16, width_at(1))
    fill(oext_cols - 16, -16, 16, width_at(-1))
    blank = jnp.zeros((oext_cols - ocols - 32, dip), jnp.bfloat16)
    k_hi[ocols + 16:oext_cols - 16, :] = blank
    k_lo[ocols + 16:oext_cols - 16, :] = blank

    picks = (lane & 3) < 2

    def assemble(t):
        ext_pack[t, 0:rows, :] = jnp.where(picks, recv_pack[1, t], recv_pack[0, t])
        few = picks[0:HALO]
        after, before = pl.ds(rows, HALO), pl.ds(ext_rows - HALO, HALO)
        ext_pack[t, after, :] = jnp.where(few, recv_corner[1, 1, t], recv_corner[1, 0, t])
        ext_pack[t, before, :] = jnp.where(few, recv_corner[0, 1, t], recv_corner[0, 0, t])
        sides = ext_pack[t]
        for f in range(ALL):
            ext[f, t + 1, :, lanes:2 * lanes] = (
                pltpu.roll(sides, lanes - 4 * f, 1) if f else sides)
        i = 0 if t < FRONT else 1
        for f, count, at in row_pieces(0, t):
            ext[f, t + 1, ext_rows - count:ext_rows, 0:lanes] = recv_rows[0, i, at:at + count, :]
        for f, count, at in row_pieces(1, t):
            ext[f, t + 1, rows:rows + count, 0:lanes] = recv_rows[1, i, at:at + count, :]

    def velocity_1(u, s11, s11_next, s12, s13):
        return ext[V1, u] + time_step * ext[BUO, u] * (
            (s11_next - s11) + (s12 - rows_down(s12)) + (s13 - lanes_down(s13)))

    def velocity(t):
        u = t + 1
        s12, s13, s23 = ext[S12, u], ext[S13, u], ext[S23, u]
        scale = time_step * ext[BUO, u]
        s22, s33 = ext[S22, u], ext[S33, u]
        ext[V1, u] = velocity_1(u, ext[S11, u], ext[S11, u + 1], s12, s13)
        ext[V2, u] = ext[V2, u] + scale * (
            (rows_up(s22) - s22) + (s12 - ext[S12, u - 1]) + (s23 - lanes_down(s23)))
        ext[V3, u] = ext[V3, u] + scale * (
            (lanes_up(s33) - s33) + (s13 - ext[S13, u - 1]) + (s23 - rows_down(s23)))

    def strains(u):
        v1, v2, v3 = ext[V1, u], ext[V2, u], ext[V3, u]
        return v1 - ext[V1, u - 1], v2 - rows_down(v2), v3 - lanes_down(v3)

    def stress_values(u):
        v1, v2, v3 = ext[V1, u], ext[V2, u], ext[V3, u]
        e1, e2, e3 = strains(u)
        scale = time_step * ext[MU, u]
        common = time_step * ext[LAM, u] * (e1 + e2 + e3)
        twice = 2.0 * scale
        return (
            (S11, ext[S11, u] + (common + twice * e1)),
            (S22, ext[S22, u] + (common + twice * e2)),
            (S33, ext[S33, u] + (common + twice * e3)),
            (S23, ext[S23, u] + scale * ((lanes_up(v2) - v2) + (rows_up(v3) - v3))),
            (S13, ext[S13, u] + scale * ((lanes_up(v1) - v1) + (ext[V3, u + 1] - v3))),
            (S12, ext[S12, u] + scale * ((rows_up(v1) - v1) + (ext[V2, u + 1] - v2))),
        )

    def stress(t):
        for f, value in stress_values(t + 1):
            ext[f, t + 1] = value

    def last_stress(t):
        for f in (V1, V2, V3):
            slab_out[f, t] = ext[f, t + 1, 0:rows, 0:lanes]
        for f, value in stress_values(t + 1):
            slab_out[f, t] = value[0:rows, 0:lanes]

    await_all(0)
    for t in range(FRONT):
        assemble(t)
    velocity(0)
    velocity(1)
    stress(0)
    e1, e2, e3 = strains(2)
    s11_next = ext[S11, 2] + time_step * (
        ext[LAM, 2] * (e1 + e2 + e3) + 2.0 * ext[MU, 2] * e1)
    second = velocity_1(1, ext[S11, 1], s11_next, ext[S12, 1], ext[S13, 1])
    rise = time_step * (ext[V1, 1] + second)
    uplift[blk] = rise[0:rows, 0:lanes]

    def up_copy(turn):
        return remote(uplift.at[blk], uplift.at[blk], up_send.at[turn], up_recv.at[turn],
                      (sec, lax.rem(blk + turn, n_blk)))

    def up_arrival(turn):
        owner = lax.rem(blk + n_blk - turn, n_blk)
        return remote(uplift.at[owner], uplift.at[owner], up_send.at[turn], up_recv.at[turn],
                      (sec, lax.rem(blk + turn, n_blk)))

    for turn in range(1, n_blk):
        up_copy(turn).start()

    await_all(1)
    for t in range(FRONT, thick):
        assemble(t)
    for t in range(2, thick):
        velocity(t)
    for t in range(1, thick):
        stress(t)

    for turn in range(1, n_blk):
        up_arrival(turn).wait_recv()
    whole = jnp.concatenate([uplift[b] for b in range(n_blk)], axis=1)
    high = whole.astype(jnp.bfloat16)
    low = (whole - high.astype(jnp.float32)).astype(jnp.bfloat16)
    dims = (((1,), (1,)), ((), ()))
    by_high = lax.dot_general(jnp.concatenate([high, low], axis=0), k_hi[...], dims,
                              preferred_element_type=jnp.float32)
    by_low = lax.dot_general(high, k_lo[...], dims, preferred_element_type=jnp.float32)
    source[OHALO:OHALO + rows, :] = by_high[0:rows] + (by_high[rows:] + by_low)

    def src_copy(d):
        out_rows = pl.ds(rows, OHALO) if d == 0 else pl.ds(OHALO, OHALO)
        to_rows = pl.ds(0, OHALO) if d == 0 else pl.ds(OHALO + rows, OHALO)
        return remote(source.at[out_rows], source.at[to_rows], src_send.at[d], src_recv.at[d],
                      (sec + SEC_DIRS[d], blk))

    for d in range(2):
        @pl.when(has_sec(SEC_DIRS[d]))
        def _():
            src_copy(d).start()

    for t in range(thick):
        velocity(t)
    for t in range(thick):
        last_stress(t)

    await_all(2)
    for d in range(2):
        @pl.when(has_sec(-SEC_DIRS[d]))
        def _():
            src_copy(d).wait_recv()

    right = (lane & 15) < 8
    side_rows = jnp.concatenate([
        jnp.where(right[0:OHALO], recv_ocorner[0, 1], recv_ocorner[0, 0]),
        jnp.where(right, recv_opack[1], recv_opack[0]),
        jnp.where(right[0:OHALO], recv_ocorner[1, 1], recv_ocorner[1, 0]),
    ], axis=0)
    for a in range(4):
        sides = pltpu.roll(side_rows, lanes - 16 * a, 1) if a else side_rows
        own = oext[a, :, 0:ocols]
        if a == 0:
            own, sides = own + source[:, 0:ocols], sides + source[:, ocols:]
        ocean_out[a, :, 0:ocols] = own
        ocean_out[a, :, ocols:] = sides

    for d in range(2):
        @pl.when(has_sec(SEC_DIRS[d]))
        def _():
            for i in range(3):
                sec_copy(d, i).wait_send()
            src_copy(d).wait_send()
        for e in range(2):
            @pl.when(both(d, e))
            def _():
                for i in range(3):
                    diag_copy(d, e, i).wait_send()
    for e in range(2):
        @pl.when(has_blk(SEC_DIRS[e]))
        def _():
            for i in range(3):
                blk_copy(e, i).wait_send()
    for turn in range(1, n_blk):
        up_copy(turn).wait_send()


def wave_body(slab, state, slab_out, ocean_out, result, slab_sem, ocean_sem):
    n_sec = lax.axis_size("sec")
    n_blk = lax.axis_size("blk")
    sec = lax.axis_index("sec")
    blk = lax.axis_index("blk")
    rows, ocols = result.shape[1:]
    all_rows, oext_cols = state.shape[1:]
    slab_copy = pltpu.make_async_copy(slab, slab_out, slab_sem)
    slab_copy.start()
    surface, flux_strike, flux_dip, still = (state[a] for a in range(4))
    row_at = lax.broadcasted_iota(jnp.int32, (all_rows, oext_cols), 0) + (sec * rows - OHALO)
    col = lax.broadcasted_iota(jnp.int32, (all_rows, oext_cols), 1)
    col_at = jnp.where(col < (ocols + oext_cols) // 2, col, col - oext_cols) + blk * ocols
    wet = ((row_at >= 0) & (row_at < n_sec * rows)) & ((col_at >= 0) & (col_at < n_blk * ocols))
    surface = jnp.where(wet, surface, 0.0)
    pull = wave_step * 0.5 * still
    for _ in range(WAVE_STEPS):
        change = (rows_up(flux_strike) - rows_down(flux_strike)) + (
            lanes_up(flux_dip) - lanes_down(flux_dip))
        surface = jnp.where(wet, surface - wave_step * 0.5 * change, 0.0)
        flux_strike = flux_strike - pull * (rows_up(surface) - rows_down(surface))
        flux_dip = flux_dip - pull * (lanes_up(surface) - lanes_down(surface))
    for a, value in enumerate((surface, flux_strike, flux_dip)):
        result[a] = value[OHALO:OHALO + rows, 0:ocols]
    ocean_copy = pltpu.make_async_copy(result, ocean_out, ocean_sem)
    ocean_copy.start()
    slab_copy.wait()
    ocean_copy.wait()


def on_device(
    slab_state, buoyancy, lame_lambda, lame_mu, face_map, band_widths, ocean_state, water_depth
):
    n_blk = lax.axis_size("blk")
    thick, rows, lanes = slab_state.shape[1:]
    ocols = ocean_state.shape[2]
    dip = face_map.shape[0]
    ext_rows = rows + 8
    oext_cols = ocols + lanes
    max_rows = max(part_rows(d, n) for d in range(2) for n in (FRONT, thick - FRONT))
    f32 = jnp.float32
    vmem = pl.BlockSpec(memory_space=pltpu.VMEM)
    hbm = pl.BlockSpec(memory_space=pltpu.HBM)
    dma = pltpu.SemaphoreType.DMA
    slab_done, state = pl.pallas_call(
        kernel_body,
        out_shape=(
            jax.ShapeDtypeStruct(slab_state.shape, f32),
            jax.ShapeDtypeStruct((4, rows + 2 * OHALO, oext_cols), f32),
        ),
        in_specs=[hbm] * 8,
        out_specs=(vmem, vmem),
        scratch_shapes=[
            pltpu.VMEM((ALL, thick + 2, ext_rows, 2 * lanes), f32),
            pltpu.VMEM((2, 2, max_rows, lanes), f32),
            pltpu.VMEM((2, 2, max_rows, lanes), f32),
            pltpu.VMEM((thick, rows, lanes), f32),
            pltpu.VMEM((2, thick, rows, lanes), f32),
            pltpu.VMEM((2, thick, HALO, lanes), f32),
            pltpu.VMEM((2, 2, thick, HALO, lanes), f32),
            pltpu.VMEM((thick, ext_rows, lanes), f32),
            pltpu.VMEM((4, rows + 2 * OHALO, oext_cols), f32),
            pltpu.VMEM((rows, lanes), f32),
            pltpu.VMEM((2, rows, lanes), f32),
            pltpu.VMEM((2, 2, OHALO, lanes), f32),
            pltpu.VMEM((1, dip), jnp.int32),
            pltpu.VMEM(band_widths.shape, jnp.int32),
            pltpu.VMEM((n_blk, rows, lanes), f32),
            pltpu.VMEM((rows + 2 * OHALO, oext_cols), f32),
            pltpu.VMEM((oext_cols, dip), jnp.bfloat16),
            pltpu.VMEM((oext_cols, dip), jnp.bfloat16),
            dma((8,)),
            dma((2, 3)), dma((2, 3)),
            dma((2, 3)), dma((2, 3)),
            dma((2, 2, 3)), dma((2, 2, 3)),
            dma((n_blk,)), dma((n_blk,)),
            dma((2,)), dma((2,)),
        ],
        compiler_params=pltpu.CompilerParams(
            collective_id=0, has_side_effects=True, vmem_limit_bytes=32 * 1024 * 1024
        ),
        cost_estimate=pl.CostEstimate(
            flops=200_000_000, bytes_accessed=2_000_000, transcendentals=500_000),
    )(
        *(pltpu.with_memory_space_constraint(x, pltpu.HBM) for x in (
            slab_state, buoyancy, lame_lambda, lame_mu, face_map.reshape(1, dip), band_widths,
            ocean_state, water_depth))
    )
    return pl.pallas_call(
        wave_body,
        out_shape=(
            jax.ShapeDtypeStruct(slab_state.shape, f32),
            jax.ShapeDtypeStruct(ocean_state.shape, f32),
        ),
        in_specs=[pl.BlockSpec(memory_space=pl.ANY), vmem],
        out_specs=(hbm, hbm),
        scratch_shapes=[pltpu.VMEM(ocean_state.shape, f32), dma, dma],
        compiler_params=pltpu.CompilerParams(vmem_limit_bytes=16 * 1024 * 1024),
    )(slab_done, state)


def solution(mesh):
    in_specs = (
        P(None, None, "sec", "blk"),
        P(None, "sec", "blk"),
        P(None, "sec", "blk"),
        P(None, "sec", "blk"),
        P(),
        P("sec", None),
        P(None, "sec", "blk"),
        P("sec", "blk"),
    )
    out_specs = (P(None, None, "sec", "blk"), P(None, "sec", "blk"))
    return jax.shard_map(
        on_device, mesh=mesh, in_specs=in_specs, out_specs=out_specs, check_vma=False
    )
```

```python
import functools
import math

import jax
import jax.numpy as jnp
from jax import lax
from jax.experimental import pallas as pl
from jax.experimental.pallas import tpu as pltpu
from jax.sharding import PartitionSpec as P

MESH = pl.DeviceIdType.MESH
WAVE_STEPS = 4
time_step = 0.25
wave_step = 0.5

V1, V2, V3, S11, S22, S33, S23, S13, S12, BUO, LAM, MU = range(12)
FIELDS = 9
ALL = 12
HALO = 2
OHALO = 8
FRONT = 3

TWO_ROWS = ((S12, S22, S23, V2, BUO), (S11, S12, S13, S22, S23, S33, V1, V3, BUO))
ONE_ROW = ((S11, S13, S33, V1, V3, LAM, MU), (V2, LAM, MU))


def per_layer(d):
    return HALO * len(TWO_ROWS[d]) + len(ONE_ROW[d])


def part_rows(d, layers):
    return -(-per_layer(d) * layers // 8) * 8


def row_pieces(d, t):
    at = (t if t < FRONT else t - FRONT) * per_layer(d)
    for f in TWO_ROWS[d]:
        yield f, HALO, at
        at += HALO
    for f in ONE_ROW[d]:
        yield f, 1, at
        at += 1

SEC_DIRS = (1, -1)


def rows_up(x):
    return pltpu.roll(x, x.shape[0] - 1, 0)


def rows_down(x):
    return pltpu.roll(x, 1, 0)


def lanes_up(x):
    return pltpu.roll(x, x.shape[1] - 1, 1)


def lanes_down(x):
    return pltpu.roll(x, 1, 1)


def kernel_body(
    slab, buoyancy, lame_lambda, lame_mu, face_hbm, bands_hbm, ocean, depth,
    slab_out, ocean_out,
    ext, send_rows, recv_rows, pack, recv_pack, send_corner, recv_corner, ext_pack,
    oext, opack, recv_opack, recv_ocorner, face_map, bands, uplift, level, k_hi, k_lo,
    load_sem, sec_send, sec_recv, blk_send, blk_recv, diag_send, diag_recv,
    up_send, up_recv, src_send, src_recv,
):
    n_sec = lax.axis_size("sec")
    n_blk = lax.axis_size("blk")
    sec = lax.axis_index("sec")
    blk = lax.axis_index("blk")
    thick, rows, lanes = slab.shape[1:]
    ext_rows = ext.shape[2]
    ocols = ocean.shape[2]
    oext_cols = oext.shape[2]
    dip = face_map.shape[1]
    tile_cols = bands.shape[1]
    front, back = pl.ds(0, FRONT), pl.ds(FRONT, thick - FRONT)

    def has_sec(step):
        return sec + step < n_sec if step > 0 else sec + step >= 0

    def has_blk(step):
        return blk + step < n_blk if step > 0 else blk + step >= 0

    own_rows, own_lanes = pl.ds(0, rows), pl.ds(0, lanes)
    ocean_rows, ocean_cols = pl.ds(OHALO, rows), pl.ds(0, ocols)
    layers = pl.ds(1, thick)
    loads = [
        (slab, ext.at[pl.ds(0, FIELDS), layers, own_rows, own_lanes]),
        (buoyancy, ext.at[BUO, layers, own_rows, own_lanes]),
        (lame_lambda, ext.at[LAM, layers, own_rows, own_lanes]),
        (lame_mu, ext.at[MU, layers, own_rows, own_lanes]),
        (face_hbm, face_map),
        (bands_hbm, bands),
        (ocean, oext.at[pl.ds(0, 3), ocean_rows, ocean_cols]),
        (depth, oext.at[3, ocean_rows, ocean_cols]),
    ]
    loads = [pltpu.make_async_copy(src, dst, load_sem.at[i]) for i, (src, dst) in enumerate(loads)]
    for load in loads:
        load.start()

    recv_rows[...] = jnp.zeros_like(recv_rows)
    recv_pack[...] = jnp.zeros_like(recv_pack)
    recv_corner[...] = jnp.zeros_like(recv_corner)
    recv_opack[...] = jnp.zeros_like(recv_opack)
    recv_ocorner[...] = jnp.zeros_like(recv_ocorner)
    for first in (0, OHALO + rows):
        level[first:first + OHALO, :] = jnp.zeros((OHALO, oext_cols), jnp.float32)
        oext[:, first:first + OHALO, 0:ocols] = jnp.zeros((4, OHALO, ocols), jnp.float32)

    barrier = pltpu.get_barrier_semaphore()

    def greet(step, turn):
        pl.semaphore_signal(
            barrier, inc=1,
            device_id=(sec + step, lax.rem(blk + turn, n_blk)), device_id_type=MESH,
        )

    for turn in range(1, n_blk):
        greet(0, turn)
    for step in SEC_DIRS:
        @pl.when(has_sec(step))
        def _():
            for turn in range(n_blk):
                greet(step, turn)

    for f in range(FIELDS):
        ext[f, 0] = jnp.zeros(ext.shape[2:], jnp.float32)
        ext[f, thick + 1] = jnp.zeros(ext.shape[2:], jnp.float32)

    def remote(src, dst, send_sem, recv_sem, target):
        return pltpu.make_async_remote_copy(
            src_ref=src, dst_ref=dst, send_sem=send_sem, recv_sem=recv_sem,
            device_id=target, device_id_type=MESH)

    def sec_copy(d, i):
        out_rows = pl.ds(rows, OHALO) if d == 0 else pl.ds(OHALO, OHALO)
        to_rows = pl.ds(0, OHALO) if d == 0 else pl.ds(OHALO + rows, OHALO)
        if i == 2:
            fluxes = pl.ds(1, 3)
            src, dst = oext.at[fluxes, out_rows, ocean_cols], oext.at[fluxes, to_rows, ocean_cols]
        else:
            part = pl.ds(0, part_rows(d, (FRONT, thick - FRONT)[i]))
            src, dst = send_rows.at[d, i, part], recv_rows.at[d, i, part]
        return remote(src, dst, sec_send.at[d, i], sec_recv.at[d, i], (sec + SEC_DIRS[d], blk))

    def blk_copy(e, i):
        if i == 2:
            src, dst = opack, recv_opack.at[e]
        else:
            part = (front, back)[i]
            src, dst = pack.at[part], recv_pack.at[e, part]
        return remote(src, dst, blk_send.at[e, i], blk_recv.at[e, i], (sec, blk + SEC_DIRS[e]))

    def diag_copy(d, e, i):
        if i == 2:
            src = opack.at[pl.ds(rows - OHALO, OHALO) if d == 0 else pl.ds(0, OHALO)]
            dst = recv_ocorner.at[d, e]
        else:
            part = (front, back)[i]
            src, dst = send_corner.at[d, part], recv_corner.at[d, e, part]
        return remote(src, dst, diag_send.at[d, e, i], diag_recv.at[d, e, i],
                      (sec + SEC_DIRS[d], blk + SEC_DIRS[e]))

    def both(d, e):
        return jnp.logical_and(has_sec(SEC_DIRS[d]), has_blk(SEC_DIRS[e]))

    def from_both(d, e):
        return jnp.logical_and(has_sec(-SEC_DIRS[d]), has_blk(-SEC_DIRS[e]))

    def send_all(i):
        for d in range(2):
            @pl.when(has_sec(SEC_DIRS[d]))
            def _():
                sec_copy(d, i).start()
        for d in range(2):
            for e in range(2):
                @pl.when(both(d, e))
                def _():
                    diag_copy(d, e, i).start()
        for e in range(2):
            @pl.when(has_blk(SEC_DIRS[e]))
            def _():
                blk_copy(e, i).start()

    def await_all(i):
        for d in range(2):
            @pl.when(has_sec(-SEC_DIRS[d]))
            def _():
                sec_copy(d, i).wait_recv()
            for e in range(2):
                @pl.when(from_both(d, e))
                def _():
                    diag_copy(d, e, i).wait_recv()
        for e in range(2):
            @pl.when(has_blk(-SEC_DIRS[e]))
            def _():
                blk_copy(e, i).wait_recv()

    lane = lax.broadcasted_iota(jnp.int32, (rows, lanes), 1)

    def pack_layer(t):
        packed = jnp.zeros((rows, lanes), jnp.float32)
        for f in range(ALL):
            value = ext[f, t + 1, 0:rows, 0:lanes]
            moved = pltpu.roll(value, 4 * f, 1) if f else value
            packed = jnp.where(((lane - 4 * f + 2) & (lanes - 1)) < 4, moved, packed)
        i = 0 if t < FRONT else 1
        for f, count, at in row_pieces(0, t):
            send_rows[0, i, at:at + count, :] = ext[f, t + 1, rows - count:rows, 0:lanes]
        for f, count, at in row_pieces(1, t):
            send_rows[1, i, at:at + count, :] = ext[f, t + 1, 0:count, 0:lanes]
        pack[t] = packed
        send_corner[0, t] = packed[rows - HALO:, :]
        send_corner[1, t] = packed[0:HALO, :]

    for load in loads[:4]:
        load.wait()
    for t in range(FRONT):
        pack_layer(t)
    near = (n_blk - 1) + sum(jnp.where(has_sec(step), n_blk, 0) for step in SEC_DIRS)
    pl.semaphore_wait(barrier, near)
    send_all(0)
    for t in range(FRONT, thick):
        pack_layer(t)
    send_all(1)

    for load in loads[4:]:
        load.wait()
    opacked = jnp.zeros((rows, lanes), jnp.float32)
    for a in range(4):
        value = oext[a, OHALO:OHALO + rows, 0:ocols]
        edges = jnp.where(lane < lanes // 2, value[:, 0:lanes], value[:, ocols - lanes:])
        moved = pltpu.roll(edges, 16 * a, 1) if a else edges
        opacked = jnp.where(((lane - 16 * a + 8) & (lanes - 1)) < 16, moved, opacked)
    opack[...] = opacked
    send_all(2)

    def width_at(step):
        total = jnp.zeros((1, 1), jnp.float32)
        for j in range(tile_cols):
            total = jnp.where(blk + step == j, bands[0:1, j:j + 1].astype(jnp.float32), total)
        return jnp.maximum(total, 1.0)

    chunk = 32
    face = face_map[...].astype(jnp.float32)
    index = lax.broadcasted_iota(jnp.int32, (chunk, dip), 0).astype(jnp.float32)
    own_column = (blk * ocols).astype(jnp.float32)

    def fill(first, column, count, width):
        distance = jnp.abs((index[0:count] + (own_column + float(column))) - face)
        decay = jnp.exp2(distance * (-math.pi / 2.0 * math.log2(math.e) / width))
        under = width + width * (decay * decay)
        guess = pl.reciprocal(under, approx=True)
        value = decay * (guess * (2.0 - under * guess))
        high = value.astype(jnp.bfloat16)
        k_hi[first:first + count, :] = high
        k_lo[first:first + count, :] = (value - high.astype(jnp.float32)).astype(jnp.bfloat16)

    here = width_at(0)
    for first in range(0, ocols, chunk):
        fill(first, first, chunk, here)
    fill(ocols, ocols, 16, width_at(1))
    fill(oext_cols - 16, -16, 16, width_at(-1))
    blank = jnp.zeros((oext_cols - ocols - 32, dip), jnp.bfloat16)
    k_hi[ocols + 16:oext_cols - 16, :] = blank
    k_lo[ocols + 16:oext_cols - 16, :] = blank

    picks = (lane & 3) < 2

    def assemble(t):
        ext_pack[t, 0:rows, :] = jnp.where(picks, recv_pack[1, t], recv_pack[0, t])
        few = picks[0:HALO]
        after, before = pl.ds(rows, HALO), pl.ds(ext_rows - HALO, HALO)
        ext_pack[t, after, :] = jnp.where(few, recv_corner[1, 1, t], recv_corner[1, 0, t])
        ext_pack[t, before, :] = jnp.where(few, recv_corner[0, 1, t], recv_corner[0, 0, t])
        sides = ext_pack[t]
        for f in range(ALL):
            ext[f, t + 1, :, lanes:2 * lanes] = (
                pltpu.roll(sides, lanes - 4 * f, 1) if f else sides)
        i = 0 if t < FRONT else 1
        for f, count, at in row_pieces(0, t):
            ext[f, t + 1, ext_rows - count:ext_rows, 0:lanes] = recv_rows[0, i, at:at + count, :]
        for f, count, at in row_pieces(1, t):
            ext[f, t + 1, rows:rows + count, 0:lanes] = recv_rows[1, i, at:at + count, :]

    def velocity_1(u, s11, s11_next, s12, s13):
        return ext[V1, u] + time_step * ext[BUO, u] * (
            (s11_next - s11) + (s12 - rows_down(s12)) + (s13 - lanes_down(s13)))

    def velocity(t):
        u = t + 1
        s12, s13, s23 = ext[S12, u], ext[S13, u], ext[S23, u]
        scale = time_step * ext[BUO, u]
        s22, s33 = ext[S22, u], ext[S33, u]
        ext[V1, u] = velocity_1(u, ext[S11, u], ext[S11, u + 1], s12, s13)
        ext[V2, u] = ext[V2, u] + scale * (
            (rows_up(s22) - s22) + (s12 - ext[S12, u - 1]) + (s23 - lanes_down(s23)))
        ext[V3, u] = ext[V3, u] + scale * (
            (lanes_up(s33) - s33) + (s13 - ext[S13, u - 1]) + (s23 - rows_down(s23)))

    def strains(u):
        v1, v2, v3 = ext[V1, u], ext[V2, u], ext[V3, u]
        return v1 - ext[V1, u - 1], v2 - rows_down(v2), v3 - lanes_down(v3)

    def stress_values(u):
        v1, v2, v3 = ext[V1, u], ext[V2, u], ext[V3, u]
        e1, e2, e3 = strains(u)
        scale = time_step * ext[MU, u]
        common = time_step * ext[LAM, u] * (e1 + e2 + e3)
        twice = 2.0 * scale
        return (
            (S11, ext[S11, u] + (common + twice * e1)),
            (S22, ext[S22, u] + (common + twice * e2)),
            (S33, ext[S33, u] + (common + twice * e3)),
            (S23, ext[S23, u] + scale * ((lanes_up(v2) - v2) + (rows_up(v3) - v3))),
            (S13, ext[S13, u] + scale * ((lanes_up(v1) - v1) + (ext[V3, u + 1] - v3))),
            (S12, ext[S12, u] + scale * ((rows_up(v1) - v1) + (ext[V2, u + 1] - v2))),
        )

    def stress(t):
        for f, value in stress_values(t + 1):
            ext[f, t + 1] = value

    def last_stress(t):
        for f in (V1, V2, V3):
            slab_out[f, t] = ext[f, t + 1, 0:rows, 0:lanes]
        for f, value in stress_values(t + 1):
            slab_out[f, t] = value[0:rows, 0:lanes]

    await_all(0)
    for t in range(FRONT):
        assemble(t)
    velocity(0)
    velocity(1)
    stress(0)
    e1, e2, e3 = strains(2)
    s11_next = ext[S11, 2] + time_step * (
        ext[LAM, 2] * (e1 + e2 + e3) + 2.0 * ext[MU, 2] * e1)
    second = velocity_1(1, ext[S11, 1], s11_next, ext[S12, 1], ext[S13, 1])
    rise = time_step * (ext[V1, 1] + second)
    uplift[blk] = rise[0:rows, 0:lanes]

    def up_copy(turn):
        return remote(uplift.at[blk], uplift.at[blk], up_send.at[turn], up_recv.at[turn],
                      (sec, lax.rem(blk + turn, n_blk)))

    def up_arrival(turn):
        owner = lax.rem(blk + n_blk - turn, n_blk)
        return remote(uplift.at[owner], uplift.at[owner], up_send.at[turn], up_recv.at[turn],
                      (sec, lax.rem(blk + turn, n_blk)))

    for turn in range(1, n_blk):
        up_copy(turn).start()

    for e in range(2):
        @pl.when(has_blk(-SEC_DIRS[e]))
        def _():
            blk_copy(e, 2).wait_recv()
    for turn in range(1, n_blk):
        up_arrival(turn).wait_recv()
    whole = jnp.concatenate([uplift[b] for b in range(n_blk)], axis=1)
    high = whole.astype(jnp.bfloat16)
    low = (whole - high.astype(jnp.float32)).astype(jnp.bfloat16)
    dims = (((1,), (1,)), ((), ()))
    by_high = lax.dot_general(jnp.concatenate([high, low], axis=0), k_hi[...], dims,
                              preferred_element_type=jnp.float32)
    by_low = lax.dot_general(high, k_lo[...], dims, preferred_element_type=jnp.float32)
    own_source = by_high[0:rows] + (by_high[rows:] + by_low)
    right = (lane & 15) < 8
    beside = jnp.where(right, recv_opack[1], recv_opack[0])
    level[OHALO:OHALO + rows, 0:ocols] = oext[0, ocean_rows, ocean_cols] + own_source[:, 0:ocols]
    level[OHALO:OHALO + rows, ocols:] = beside + own_source[:, ocols:]

    def src_copy(d):
        out_rows = pl.ds(rows, OHALO) if d == 0 else pl.ds(OHALO, OHALO)
        to_rows = pl.ds(0, OHALO) if d == 0 else pl.ds(OHALO + rows, OHALO)
        return remote(level.at[out_rows], level.at[to_rows], src_send.at[d], src_recv.at[d],
                      (sec + SEC_DIRS[d], blk))

    for d in range(2):
        @pl.when(has_sec(SEC_DIRS[d]))
        def _():
            src_copy(d).start()

    await_all(1)
    for t in range(FRONT, thick):
        assemble(t)
    for t in range(2, thick):
        velocity(t)
    for t in range(1, thick):
        stress(t)

    for t in range(thick):
        velocity(t)
    for t in range(thick):
        last_stress(t)

    for d in range(2):
        @pl.when(has_sec(-SEC_DIRS[d]))
        def _():
            sec_copy(d, 2).wait_recv()
        for e in range(2):
            @pl.when(from_both(d, e))
            def _():
                diag_copy(d, e, 2).wait_recv()
    for d in range(2):
        @pl.when(has_sec(-SEC_DIRS[d]))
        def _():
            src_copy(d).wait_recv()

    side_rows = jnp.concatenate([
        jnp.where(right[0:OHALO], recv_ocorner[0, 1], recv_ocorner[0, 0]),
        beside,
        jnp.where(right[0:OHALO], recv_ocorner[1, 1], recv_ocorner[1, 0]),
    ], axis=0)
    ocean_out[0] = level[...]
    for a in range(1, 4):
        ocean_out[a, :, 0:ocols] = oext[a, :, 0:ocols]
        ocean_out[a, :, ocols:] = pltpu.roll(side_rows, lanes - 16 * a, 1)

    for d in range(2):
        @pl.when(has_sec(SEC_DIRS[d]))
        def _():
            for i in range(3):
                sec_copy(d, i).wait_send()
            src_copy(d).wait_send()
        for e in range(2):
            @pl.when(both(d, e))
            def _():
                for i in range(3):
                    diag_copy(d, e, i).wait_send()
    for e in range(2):
        @pl.when(has_blk(SEC_DIRS[e]))
        def _():
            for i in range(3):
                blk_copy(e, i).wait_send()
    for turn in range(1, n_blk):
        up_copy(turn).wait_send()


def wave_body(slab, state, slab_out, ocean_out, result, slab_sem, ocean_sem):
    n_sec = lax.axis_size("sec")
    n_blk = lax.axis_size("blk")
    sec = lax.axis_index("sec")
    blk = lax.axis_index("blk")
    rows, ocols = result.shape[1:]
    all_rows, oext_cols = state.shape[1:]
    slab_copy = pltpu.make_async_copy(slab, slab_out, slab_sem)
    slab_copy.start()
    surface, flux_strike, flux_dip, still = (state[a] for a in range(4))
    row_at = lax.broadcasted_iota(jnp.int32, (all_rows, oext_cols), 0) + (sec * rows - OHALO)
    col = lax.broadcasted_iota(jnp.int32, (all_rows, oext_cols), 1)
    col_at = jnp.where(col < (ocols + oext_cols) // 2, col, col - oext_cols) + blk * ocols
    wet = ((row_at >= 0) & (row_at < n_sec * rows)) & ((col_at >= 0) & (col_at < n_blk * ocols))
    surface = jnp.where(wet, surface, 0.0)
    pull = wave_step * 0.5 * still
    for _ in range(WAVE_STEPS):
        change = (rows_up(flux_strike) - rows_down(flux_strike)) + (
            lanes_up(flux_dip) - lanes_down(flux_dip))
        surface = jnp.where(wet, surface - wave_step * 0.5 * change, 0.0)
        flux_strike = flux_strike - pull * (rows_up(surface) - rows_down(surface))
        flux_dip = flux_dip - pull * (lanes_up(surface) - lanes_down(surface))
    for a, value in enumerate((surface, flux_strike, flux_dip)):
        result[a] = value[OHALO:OHALO + rows, 0:ocols]
    ocean_copy = pltpu.make_async_copy(result, ocean_out, ocean_sem)
    ocean_copy.start()
    slab_copy.wait()
    ocean_copy.wait()


def on_device(
    slab_state, buoyancy, lame_lambda, lame_mu, face_map, band_widths, ocean_state, water_depth
):
    n_blk = lax.axis_size("blk")
    thick, rows, lanes = slab_state.shape[1:]
    ocols = ocean_state.shape[2]
    dip = face_map.shape[0]
    ext_rows = rows + 8
    oext_cols = ocols + lanes
    max_rows = max(part_rows(d, n) for d in range(2) for n in (FRONT, thick - FRONT))
    f32 = jnp.float32
    vmem = pl.BlockSpec(memory_space=pltpu.VMEM)
    hbm = pl.BlockSpec(memory_space=pltpu.HBM)
    dma = pltpu.SemaphoreType.DMA
    slab_done, state = pl.pallas_call(
        kernel_body,
        out_shape=(
            jax.ShapeDtypeStruct(slab_state.shape, f32),
            jax.ShapeDtypeStruct((4, rows + 2 * OHALO, oext_cols), f32),
        ),
        in_specs=[hbm] * 8,
        out_specs=(vmem, vmem),
        scratch_shapes=[
            pltpu.VMEM((ALL, thick + 2, ext_rows, 2 * lanes), f32),
            pltpu.VMEM((2, 2, max_rows, lanes), f32),
            pltpu.VMEM((2, 2, max_rows, lanes), f32),
            pltpu.VMEM((thick, rows, lanes), f32),
            pltpu.VMEM((2, thick, rows, lanes), f32),
            pltpu.VMEM((2, thick, HALO, lanes), f32),
            pltpu.VMEM((2, 2, thick, HALO, lanes), f32),
            pltpu.VMEM((thick, ext_rows, lanes), f32),
            pltpu.VMEM((4, rows + 2 * OHALO, oext_cols), f32),
            pltpu.VMEM((rows, lanes), f32),
            pltpu.VMEM((2, rows, lanes), f32),
            pltpu.VMEM((2, 2, OHALO, lanes), f32),
            pltpu.VMEM((1, dip), jnp.int32),
            pltpu.VMEM(band_widths.shape, jnp.int32),
            pltpu.VMEM((n_blk, rows, lanes), f32),
            pltpu.VMEM((rows + 2 * OHALO, oext_cols), f32),
            pltpu.VMEM((oext_cols, dip), jnp.bfloat16),
            pltpu.VMEM((oext_cols, dip), jnp.bfloat16),
            dma((8,)),
            dma((2, 3)), dma((2, 3)),
            dma((2, 3)), dma((2, 3)),
            dma((2, 2, 3)), dma((2, 2, 3)),
            dma((n_blk,)), dma((n_blk,)),
            dma((2,)), dma((2,)),
        ],
        compiler_params=pltpu.CompilerParams(
            collective_id=0, has_side_effects=True, vmem_limit_bytes=32 * 1024 * 1024
        ),
        cost_estimate=pl.CostEstimate(
            flops=200_000_000, bytes_accessed=2_000_000, transcendentals=500_000),
    )(
        *(pltpu.with_memory_space_constraint(x, pltpu.HBM) for x in (
            slab_state, buoyancy, lame_lambda, lame_mu, face_map.reshape(1, dip), band_widths,
            ocean_state, water_depth))
    )
    return pl.pallas_call(
        wave_body,
        out_shape=(
            jax.ShapeDtypeStruct(slab_state.shape, f32),
            jax.ShapeDtypeStruct(ocean_state.shape, f32),
        ),
        in_specs=[pl.BlockSpec(memory_space=pl.ANY), vmem],
        out_specs=(hbm, hbm),
        scratch_shapes=[pltpu.VMEM(ocean_state.shape, f32), dma, dma],
        compiler_params=pltpu.CompilerParams(vmem_limit_bytes=16 * 1024 * 1024),
    )(slab_done, state)


def solution(mesh):
    in_specs = (
        P(None, None, "sec", "blk"),
        P(None, "sec", "blk"),
        P(None, "sec", "blk"),
        P(None, "sec", "blk"),
        P(),
        P("sec", None),
        P(None, "sec", "blk"),
        P("sec", "blk"),
    )
    out_specs = (P(None, None, "sec", "blk"), P(None, "sec", "blk"))
    return jax.shard_map(
        on_device, mesh=mesh, in_specs=in_specs, out_specs=out_specs, check_vma=False
    )
```

```python
import functools
import math

import jax
import jax.numpy as jnp
from jax import lax
from jax.experimental import pallas as pl
from jax.experimental.pallas import tpu as pltpu
from jax.sharding import PartitionSpec as P

MESH = pl.DeviceIdType.MESH
WAVE_STEPS = 4
time_step = 0.25
wave_step = 0.5

V1, V2, V3, S11, S22, S33, S23, S13, S12, BUO, LAM, MU = range(12)
FIELDS = 9
ALL = 12
HALO = 2
OHALO = 8
FRONT = 3

TWO_ROWS = ((S12, S22, S23, V2, BUO), (S11, S12, S13, S22, S23, S33, V1, V3, BUO))
ONE_ROW = ((S11, S13, S33, V1, V3, LAM, MU), (V2, LAM, MU))


def per_layer(d):
    return HALO * len(TWO_ROWS[d]) + len(ONE_ROW[d])


def part_rows(d, layers):
    return -(-per_layer(d) * layers // 8) * 8


def row_pieces(d, t):
    at = (t if t < FRONT else t - FRONT) * per_layer(d)
    for f in TWO_ROWS[d]:
        yield f, HALO, at
        at += HALO
    for f in ONE_ROW[d]:
        yield f, 1, at
        at += 1

SEC_DIRS = (1, -1)


def rows_up(x):
    return pltpu.roll(x, x.shape[0] - 1, 0)


def rows_down(x):
    return pltpu.roll(x, 1, 0)


def lanes_up(x):
    return pltpu.roll(x, x.shape[1] - 1, 1)


def lanes_down(x):
    return pltpu.roll(x, 1, 1)


def kernel_body(
    slab, buoyancy, lame_lambda, lame_mu, face_hbm, bands_hbm, ocean, depth,
    slab_out, ocean_out,
    ext, send_rows, recv_rows, pack, recv_pack, send_corner, recv_corner, ext_pack,
    oext, opack, recv_opack, recv_ocorner, face_map, bands, uplift, level, k_hi, k_lo,
    load_sem, sec_send, sec_recv, blk_send, blk_recv, diag_send, diag_recv,
    up_send, up_recv, src_send, src_recv,
):
    n_sec = lax.axis_size("sec")
    n_blk = lax.axis_size("blk")
    sec = lax.axis_index("sec")
    blk = lax.axis_index("blk")
    thick, rows, lanes = slab.shape[1:]
    ext_rows = ext.shape[2]
    ocols = ocean.shape[2]
    oext_cols = oext.shape[2]
    dip = face_map.shape[1]
    tile_cols = bands.shape[1]
    front, back = pl.ds(0, FRONT), pl.ds(FRONT, thick - FRONT)

    def has_sec(step):
        return sec + step < n_sec if step > 0 else sec + step >= 0

    def has_blk(step):
        return blk + step < n_blk if step > 0 else blk + step >= 0

    own_rows, own_lanes = pl.ds(0, rows), pl.ds(0, lanes)
    ocean_rows, ocean_cols = pl.ds(OHALO, rows), pl.ds(0, ocols)
    layers = pl.ds(1, thick)
    loads = [
        (slab, ext.at[pl.ds(0, FIELDS), layers, own_rows, own_lanes]),
        (buoyancy, ext.at[BUO, layers, own_rows, own_lanes]),
        (lame_lambda, ext.at[LAM, layers, own_rows, own_lanes]),
        (lame_mu, ext.at[MU, layers, own_rows, own_lanes]),
        (face_hbm, face_map),
        (bands_hbm, bands),
        (ocean, oext.at[pl.ds(0, 3), ocean_rows, ocean_cols]),
        (depth, oext.at[3, ocean_rows, ocean_cols]),
    ]
    loads = [pltpu.make_async_copy(src, dst, load_sem.at[i]) for i, (src, dst) in enumerate(loads)]
    for load in loads:
        load.start()

    recv_rows[...] = jnp.zeros_like(recv_rows)
    recv_pack[...] = jnp.zeros_like(recv_pack)
    recv_corner[...] = jnp.zeros_like(recv_corner)
    recv_opack[...] = jnp.zeros_like(recv_opack)
    recv_ocorner[...] = jnp.zeros_like(recv_ocorner)
    for first in (0, OHALO + rows):
        level[first:first + OHALO, :] = jnp.zeros((OHALO, oext_cols), jnp.float32)
        oext[:, first:first + OHALO, 0:ocols] = jnp.zeros((4, OHALO, ocols), jnp.float32)

    barrier = pltpu.get_barrier_semaphore()

    def greet(step, turn):
        pl.semaphore_signal(
            barrier, inc=1,
            device_id=(sec + step, lax.rem(blk + turn, n_blk)), device_id_type=MESH,
        )

    for turn in range(1, n_blk):
        greet(0, turn)
    for step in SEC_DIRS:
        @pl.when(has_sec(step))
        def _():
            for turn in range(n_blk):
                greet(step, turn)

    for f in range(FIELDS):
        ext[f, 0] = jnp.zeros(ext.shape[2:], jnp.float32)
        ext[f, thick + 1] = jnp.zeros(ext.shape[2:], jnp.float32)

    def remote(src, dst, send_sem, recv_sem, target):
        return pltpu.make_async_remote_copy(
            src_ref=src, dst_ref=dst, send_sem=send_sem, recv_sem=recv_sem,
            device_id=target, device_id_type=MESH)

    def sec_copy(d, i):
        out_rows = pl.ds(rows, OHALO) if d == 0 else pl.ds(OHALO, OHALO)
        to_rows = pl.ds(0, OHALO) if d == 0 else pl.ds(OHALO + rows, OHALO)
        if i == 2:
            fluxes = pl.ds(1, 3)
            src, dst = oext.at[fluxes, out_rows, ocean_cols], oext.at[fluxes, to_rows, ocean_cols]
        else:
            part = pl.ds(0, part_rows(d, (FRONT, thick - FRONT)[i]))
            src, dst = send_rows.at[d, i, part], recv_rows.at[d, i, part]
        return remote(src, dst, sec_send.at[d, i], sec_recv.at[d, i], (sec + SEC_DIRS[d], blk))

    def blk_copy(e, i):
        if i == 2:
            src, dst = opack, recv_opack.at[e]
        else:
            part = (front, back)[i]
            src, dst = pack.at[part], recv_pack.at[e, part]
        return remote(src, dst, blk_send.at[e, i], blk_recv.at[e, i], (sec, blk + SEC_DIRS[e]))

    def diag_copy(d, e, i):
        if i == 2:
            src = opack.at[pl.ds(rows - OHALO, OHALO) if d == 0 else pl.ds(0, OHALO)]
            dst = recv_ocorner.at[d, e]
        else:
            part = (front, back)[i]
            src, dst = send_corner.at[d, part], recv_corner.at[d, e, part]
        return remote(src, dst, diag_send.at[d, e, i], diag_recv.at[d, e, i],
                      (sec + SEC_DIRS[d], blk + SEC_DIRS[e]))

    def both(d, e):
        return jnp.logical_and(has_sec(SEC_DIRS[d]), has_blk(SEC_DIRS[e]))

    def from_both(d, e):
        return jnp.logical_and(has_sec(-SEC_DIRS[d]), has_blk(-SEC_DIRS[e]))

    def send_all(i):
        for d in range(2):
            @pl.when(has_sec(SEC_DIRS[d]))
            def _():
                sec_copy(d, i).start()
        for d in range(2):
            for e in range(2):
                @pl.when(both(d, e))
                def _():
                    diag_copy(d, e, i).start()
        for e in range(2):
            @pl.when(has_blk(SEC_DIRS[e]))
            def _():
                blk_copy(e, i).start()

    def await_all(i):
        for d in range(2):
            @pl.when(has_sec(-SEC_DIRS[d]))
            def _():
                sec_copy(d, i).wait_recv()
            for e in range(2):
                @pl.when(from_both(d, e))
                def _():
                    diag_copy(d, e, i).wait_recv()
        for e in range(2):
            @pl.when(has_blk(-SEC_DIRS[e]))
            def _():
                blk_copy(e, i).wait_recv()

    lane = lax.broadcasted_iota(jnp.int32, (rows, lanes), 1)

    def pack_layer(t):
        packed = jnp.zeros((rows, lanes), jnp.float32)
        for f in range(ALL):
            value = ext[f, t + 1, 0:rows, 0:lanes]
            moved = pltpu.roll(value, 4 * f, 1) if f else value
            packed = jnp.where(((lane - 4 * f + 2) & (lanes - 1)) < 4, moved, packed)
        i = 0 if t < FRONT else 1
        for f, count, at in row_pieces(0, t):
            send_rows[0, i, at:at + count, :] = ext[f, t + 1, rows - count:rows, 0:lanes]
        for f, count, at in row_pieces(1, t):
            send_rows[1, i, at:at + count, :] = ext[f, t + 1, 0:count, 0:lanes]
        pack[t] = packed
        send_corner[0, t] = packed[rows - HALO:, :]
        send_corner[1, t] = packed[0:HALO, :]

    for load in loads[:4]:
        load.wait()
    for t in range(FRONT):
        pack_layer(t)
    near = (n_blk - 1) + sum(jnp.where(has_sec(step), n_blk, 0) for step in SEC_DIRS)
    pl.semaphore_wait(barrier, near)
    send_all(0)
    for t in range(FRONT, thick):
        pack_layer(t)
    send_all(1)

    for load in loads[4:]:
        load.wait()
    opacked = jnp.zeros((rows, lanes), jnp.float32)
    for a in range(4):
        value = oext[a, OHALO:OHALO + rows, 0:ocols]
        edges = jnp.where(lane < lanes // 2, value[:, 0:lanes], value[:, ocols - lanes:])
        moved = pltpu.roll(edges, 16 * a, 1) if a else edges
        opacked = jnp.where(((lane - 16 * a + 8) & (lanes - 1)) < 16, moved, opacked)
    opack[...] = opacked
    send_all(2)

    def width_at(step):
        total = jnp.zeros((1, 1), jnp.float32)
        for j in range(tile_cols):
            total = jnp.where(blk + step == j, bands[0:1, j:j + 1].astype(jnp.float32), total)
        return jnp.maximum(total, 1.0)

    chunk = 64
    face = face_map[...].astype(jnp.float32)
    index = lax.broadcasted_iota(jnp.int32, (chunk, dip), 0).astype(jnp.float32)
    own_column = (blk * ocols).astype(jnp.float32)

    def fill(first, column, count, width):
        distance = jnp.abs((index[0:count] + column) - face)
        decay = jnp.exp2(distance * (-math.pi / 2.0 * math.log2(math.e) / width))
        under = width + width * (decay * decay)
        guess = pl.reciprocal(under, approx=True)
        value = decay * (guess * (2.0 - under * guess))
        high = value.astype(jnp.bfloat16)
        k_hi[pl.ds(first, count), :] = high
        k_lo[pl.ds(first, count), :] = (value - high.astype(jnp.float32)).astype(jnp.bfloat16)

    here = width_at(0)

    def fill_chunk(i, carry):
        first = pl.multiple_of(i * chunk, chunk)
        fill(first, own_column + first.astype(jnp.float32), chunk, here)
        return carry

    lax.fori_loop(0, ocols // chunk, fill_chunk, 0)
    fill(ocols, own_column + float(ocols), 16, width_at(1))
    fill(oext_cols - 16, own_column - 16.0, 16, width_at(-1))
    blank = jnp.zeros((oext_cols - ocols - 32, dip), jnp.bfloat16)
    k_hi[ocols + 16:oext_cols - 16, :] = blank
    k_lo[ocols + 16:oext_cols - 16, :] = blank

    picks = (lane & 3) < 2

    def assemble(t):
        ext_pack[t, 0:rows, :] = jnp.where(picks, recv_pack[1, t], recv_pack[0, t])
        few = picks[0:HALO]
        after, before = pl.ds(rows, HALO), pl.ds(ext_rows - HALO, HALO)
        ext_pack[t, after, :] = jnp.where(few, recv_corner[1, 1, t], recv_corner[1, 0, t])
        ext_pack[t, before, :] = jnp.where(few, recv_corner[0, 1, t], recv_corner[0, 0, t])
        sides = ext_pack[t]
        for f in range(ALL):
            ext[f, t + 1, :, lanes:2 * lanes] = (
                pltpu.roll(sides, lanes - 4 * f, 1) if f else sides)
        i = 0 if t < FRONT else 1
        for f, count, at in row_pieces(0, t):
            ext[f, t + 1, ext_rows - count:ext_rows, 0:lanes] = recv_rows[0, i, at:at + count, :]
        for f, count, at in row_pieces(1, t):
            ext[f, t + 1, rows:rows + count, 0:lanes] = recv_rows[1, i, at:at + count, :]

    def velocity_1(u, s11, s11_next, s12, s13):
        return ext[V1, u] + time_step * ext[BUO, u] * (
            (s11_next - s11) + (s12 - rows_down(s12)) + (s13 - lanes_down(s13)))

    def velocity(t):
        u = t + 1
        s12, s13, s23 = ext[S12, u], ext[S13, u], ext[S23, u]
        scale = time_step * ext[BUO, u]
        s22, s33 = ext[S22, u], ext[S33, u]
        ext[V1, u] = velocity_1(u, ext[S11, u], ext[S11, u + 1], s12, s13)
        ext[V2, u] = ext[V2, u] + scale * (
            (rows_up(s22) - s22) + (s12 - ext[S12, u - 1]) + (s23 - lanes_down(s23)))
        ext[V3, u] = ext[V3, u] + scale * (
            (lanes_up(s33) - s33) + (s13 - ext[S13, u - 1]) + (s23 - rows_down(s23)))

    def strains(u):
        v1, v2, v3 = ext[V1, u], ext[V2, u], ext[V3, u]
        return v1 - ext[V1, u - 1], v2 - rows_down(v2), v3 - lanes_down(v3)

    def stress_values(u):
        v1, v2, v3 = ext[V1, u], ext[V2, u], ext[V3, u]
        e1, e2, e3 = strains(u)
        scale = time_step * ext[MU, u]
        common = time_step * ext[LAM, u] * (e1 + e2 + e3)
        twice = 2.0 * scale
        return (
            (S11, ext[S11, u] + (common + twice * e1)),
            (S22, ext[S22, u] + (common + twice * e2)),
            (S33, ext[S33, u] + (common + twice * e3)),
            (S23, ext[S23, u] + scale * ((lanes_up(v2) - v2) + (rows_up(v3) - v3))),
            (S13, ext[S13, u] + scale * ((lanes_up(v1) - v1) + (ext[V3, u + 1] - v3))),
            (S12, ext[S12, u] + scale * ((rows_up(v1) - v1) + (ext[V2, u + 1] - v2))),
        )

    def stress(t):
        for f, value in stress_values(t + 1):
            ext[f, t + 1] = value

    def last_stress(t):
        for f in (V1, V2, V3):
            slab_out[f, t] = ext[f, t + 1, 0:rows, 0:lanes]
        for f, value in stress_values(t + 1):
            slab_out[f, t] = value[0:rows, 0:lanes]

    def layers_in_turn(first, end, step):
        def two(i, carry):
            step(first + 2 * i)
            step(first + 2 * i + 1)
            return carry

        lax.fori_loop(0, (end - first) // 2, two, 0)

    await_all(0)
    for t in range(FRONT):
        assemble(t)
    velocity(0)
    velocity(1)
    stress(0)
    e1, e2, e3 = strains(2)
    s11_next = ext[S11, 2] + time_step * (
        ext[LAM, 2] * (e1 + e2 + e3) + 2.0 * ext[MU, 2] * e1)
    second = velocity_1(1, ext[S11, 1], s11_next, ext[S12, 1], ext[S13, 1])
    rise = time_step * (ext[V1, 1] + second)
    uplift[blk] = rise[0:rows, 0:lanes]

    def up_copy(turn):
        return remote(uplift.at[blk], uplift.at[blk], up_send.at[turn], up_recv.at[turn],
                      (sec, lax.rem(blk + turn, n_blk)))

    def up_arrival(turn):
        owner = lax.rem(blk + n_blk - turn, n_blk)
        return remote(uplift.at[owner], uplift.at[owner], up_send.at[turn], up_recv.at[turn],
                      (sec, lax.rem(blk + turn, n_blk)))

    for turn in range(1, n_blk):
        up_copy(turn).start()

    for e in range(2):
        @pl.when(has_blk(-SEC_DIRS[e]))
        def _():
            blk_copy(e, 2).wait_recv()
    for turn in range(1, n_blk):
        up_arrival(turn).wait_recv()
    whole = jnp.concatenate([uplift[b] for b in range(n_blk)], axis=1)
    high = whole.astype(jnp.bfloat16)
    low = (whole - high.astype(jnp.float32)).astype(jnp.bfloat16)
    dims = (((1,), (1,)), ((), ()))
    by_high = lax.dot_general(jnp.concatenate([high, low], axis=0), k_hi[...], dims,
                              preferred_element_type=jnp.float32)
    by_low = lax.dot_general(high, k_lo[...], dims, preferred_element_type=jnp.float32)
    own_source = by_high[0:rows] + (by_high[rows:] + by_low)
    right = (lane & 15) < 8
    beside = jnp.where(right, recv_opack[1], recv_opack[0])
    level[OHALO:OHALO + rows, 0:ocols] = oext[0, ocean_rows, ocean_cols] + own_source[:, 0:ocols]
    level[OHALO:OHALO + rows, ocols:] = beside + own_source[:, ocols:]

    def src_copy(d):
        out_rows = pl.ds(rows, OHALO) if d == 0 else pl.ds(OHALO, OHALO)
        to_rows = pl.ds(0, OHALO) if d == 0 else pl.ds(OHALO + rows, OHALO)
        return remote(level.at[out_rows], level.at[to_rows], src_send.at[d], src_recv.at[d],
                      (sec + SEC_DIRS[d], blk))

    for d in range(2):
        @pl.when(has_sec(SEC_DIRS[d]))
        def _():
            src_copy(d).start()

    await_all(1)
    for t in range(FRONT, thick):
        assemble(t)
    layers_in_turn(2, thick, velocity)
    stress(1)
    layers_in_turn(2, thick, stress)

    layers_in_turn(0, thick, velocity)
    layers_in_turn(0, thick, last_stress)

    for d in range(2):
        @pl.when(has_sec(-SEC_DIRS[d]))
        def _():
            sec_copy(d, 2).wait_recv()
        for e in range(2):
            @pl.when(from_both(d, e))
            def _():
                diag_copy(d, e, 2).wait_recv()
    for d in range(2):
        @pl.when(has_sec(-SEC_DIRS[d]))
        def _():
            src_copy(d).wait_recv()

    side_rows = jnp.concatenate([
        jnp.where(right[0:OHALO], recv_ocorner[0, 1], recv_ocorner[0, 0]),
        beside,
        jnp.where(right[0:OHALO], recv_ocorner[1, 1], recv_ocorner[1, 0]),
    ], axis=0)
    ocean_out[0] = level[...]
    for a in range(1, 4):
        ocean_out[a, :, 0:ocols] = oext[a, :, 0:ocols]
        ocean_out[a, :, ocols:] = pltpu.roll(side_rows, lanes - 16 * a, 1)

    for d in range(2):
        @pl.when(has_sec(SEC_DIRS[d]))
        def _():
            for i in range(3):
                sec_copy(d, i).wait_send()
            src_copy(d).wait_send()
        for e in range(2):
            @pl.when(both(d, e))
            def _():
                for i in range(3):
                    diag_copy(d, e, i).wait_send()
    for e in range(2):
        @pl.when(has_blk(SEC_DIRS[e]))
        def _():
            for i in range(3):
                blk_copy(e, i).wait_send()
    for turn in range(1, n_blk):
        up_copy(turn).wait_send()


def wave_body(slab, state, slab_out, ocean_out, result, slab_sem, ocean_sem):
    n_sec = lax.axis_size("sec")
    n_blk = lax.axis_size("blk")
    sec = lax.axis_index("sec")
    blk = lax.axis_index("blk")
    rows, ocols = result.shape[1:]
    all_rows, oext_cols = state.shape[1:]
    slab_copy = pltpu.make_async_copy(slab, slab_out, slab_sem)
    slab_copy.start()
    surface, flux_strike, flux_dip, still = (state[a] for a in range(4))
    row_at = lax.broadcasted_iota(jnp.int32, (all_rows, oext_cols), 0) + (sec * rows - OHALO)
    col = lax.broadcasted_iota(jnp.int32, (all_rows, oext_cols), 1)
    col_at = jnp.where(col < (ocols + oext_cols) // 2, col, col - oext_cols) + blk * ocols
    wet = ((row_at >= 0) & (row_at < n_sec * rows)) & ((col_at >= 0) & (col_at < n_blk * ocols))
    surface = jnp.where(wet, surface, 0.0)
    pull = wave_step * 0.5 * still
    for _ in range(WAVE_STEPS):
        change = (rows_up(flux_strike) - rows_down(flux_strike)) + (
            lanes_up(flux_dip) - lanes_down(flux_dip))
        surface = jnp.where(wet, surface - wave_step * 0.5 * change, 0.0)
        flux_strike = flux_strike - pull * (rows_up(surface) - rows_down(surface))
        flux_dip = flux_dip - pull * (lanes_up(surface) - lanes_down(surface))
    for a, value in enumerate((surface, flux_strike, flux_dip)):
        result[a] = value[OHALO:OHALO + rows, 0:ocols]
    ocean_copy = pltpu.make_async_copy(result, ocean_out, ocean_sem)
    ocean_copy.start()
    slab_copy.wait()
    ocean_copy.wait()


def on_device(
    slab_state, buoyancy, lame_lambda, lame_mu, face_map, band_widths, ocean_state, water_depth
):
    n_blk = lax.axis_size("blk")
    thick, rows, lanes = slab_state.shape[1:]
    ocols = ocean_state.shape[2]
    dip = face_map.shape[0]
    ext_rows = rows + 8
    oext_cols = ocols + lanes
    max_rows = max(part_rows(d, n) for d in range(2) for n in (FRONT, thick - FRONT))
    f32 = jnp.float32
    vmem = pl.BlockSpec(memory_space=pltpu.VMEM)
    hbm = pl.BlockSpec(memory_space=pltpu.HBM)
    dma = pltpu.SemaphoreType.DMA
    slab_done, state = pl.pallas_call(
        kernel_body,
        out_shape=(
            jax.ShapeDtypeStruct(slab_state.shape, f32),
            jax.ShapeDtypeStruct((4, rows + 2 * OHALO, oext_cols), f32),
        ),
        in_specs=[hbm] * 8,
        out_specs=(vmem, vmem),
        scratch_shapes=[
            pltpu.VMEM((ALL, thick + 2, ext_rows, 2 * lanes), f32),
            pltpu.VMEM((2, 2, max_rows, lanes), f32),
            pltpu.VMEM((2, 2, max_rows, lanes), f32),
            pltpu.VMEM((thick, rows, lanes), f32),
            pltpu.VMEM((2, thick, rows, lanes), f32),
            pltpu.VMEM((2, thick, HALO, lanes), f32),
            pltpu.VMEM((2, 2, thick, HALO, lanes), f32),
            pltpu.VMEM((thick, ext_rows, lanes), f32),
            pltpu.VMEM((4, rows + 2 * OHALO, oext_cols), f32),
            pltpu.VMEM((rows, lanes), f32),
            pltpu.VMEM((2, rows, lanes), f32),
            pltpu.VMEM((2, 2, OHALO, lanes), f32),
            pltpu.VMEM((1, dip), jnp.int32),
            pltpu.VMEM(band_widths.shape, jnp.int32),
            pltpu.VMEM((n_blk, rows, lanes), f32),
            pltpu.VMEM((rows + 2 * OHALO, oext_cols), f32),
            pltpu.VMEM((oext_cols, dip), jnp.bfloat16),
            pltpu.VMEM((oext_cols, dip), jnp.bfloat16),
            dma((8,)),
            dma((2, 3)), dma((2, 3)),
            dma((2, 3)), dma((2, 3)),
            dma((2, 2, 3)), dma((2, 2, 3)),
            dma((n_blk,)), dma((n_blk,)),
            dma((2,)), dma((2,)),
        ],
        compiler_params=pltpu.CompilerParams(
            collective_id=0, has_side_effects=True, vmem_limit_bytes=32 * 1024 * 1024
        ),
        cost_estimate=pl.CostEstimate(
            flops=200_000_000, bytes_accessed=2_000_000, transcendentals=500_000),
    )(
        *(pltpu.with_memory_space_constraint(x, pltpu.HBM) for x in (
            slab_state, buoyancy, lame_lambda, lame_mu, face_map.reshape(1, dip), band_widths,
            ocean_state, water_depth))
    )
    return pl.pallas_call(
        wave_body,
        out_shape=(
            jax.ShapeDtypeStruct(slab_state.shape, f32),
            jax.ShapeDtypeStruct(ocean_state.shape, f32),
        ),
        in_specs=[pl.BlockSpec(memory_space=pl.ANY), vmem],
        out_specs=(hbm, hbm),
        scratch_shapes=[pltpu.VMEM(ocean_state.shape, f32), dma, dma],
        compiler_params=pltpu.CompilerParams(vmem_limit_bytes=16 * 1024 * 1024),
    )(slab_done, state)


def solution(mesh):
    in_specs = (
        P(None, None, "sec", "blk"),
        P(None, "sec", "blk"),
        P(None, "sec", "blk"),
        P(None, "sec", "blk"),
        P(),
        P("sec", None),
        P(None, "sec", "blk"),
        P("sec", "blk"),
    )
    out_specs = (P(None, None, "sec", "blk"), P(None, "sec", "blk"))
    return jax.shard_map(
        on_device, mesh=mesh, in_specs=in_specs, out_specs=out_specs, check_vma=False
    )
```

```python
import functools
import math

import jax
import jax.numpy as jnp
from jax import lax
from jax.experimental import pallas as pl
from jax.experimental.pallas import tpu as pltpu
from jax.sharding import PartitionSpec as P

MESH = pl.DeviceIdType.MESH
WAVE_STEPS = 4
time_step = 0.25
wave_step = 0.5

V1, V2, V3, S11, S22, S33, S23, S13, S12, BUO, LAM, MU = range(12)
FIELDS = 9
ALL = 12
HALO = 2
OHALO = 8
FRONT = 3

TWO_ROWS = ((S12, S22, S23, V2, BUO), (S11, S12, S13, S22, S23, S33, V1, V3, BUO))
ONE_ROW = ((S11, S13, S33, V1, V3, LAM, MU), (V2, LAM, MU))


def per_layer(d):
    return HALO * len(TWO_ROWS[d]) + len(ONE_ROW[d])


def part_rows(d, layers):
    return -(-per_layer(d) * layers // 8) * 8


def row_pieces(d, t):
    at = (t if t < FRONT else t - FRONT) * per_layer(d)
    for f in TWO_ROWS[d]:
        yield f, HALO, at
        at += HALO
    for f in ONE_ROW[d]:
        yield f, 1, at
        at += 1

SEC_DIRS = (1, -1)


def rows_up(x):
    return pltpu.roll(x, x.shape[0] - 1, 0)


def rows_down(x):
    return pltpu.roll(x, 1, 0)


def lanes_up(x):
    return pltpu.roll(x, x.shape[1] - 1, 1)


def lanes_down(x):
    return pltpu.roll(x, 1, 1)


def kernel_body(
    slab, buoyancy, lame_lambda, lame_mu, face_hbm, bands_hbm, ocean, depth,
    slab_out, ocean_out,
    ext, send_rows, recv_rows, pack, recv_pack, send_corner, recv_corner, ext_pack,
    oext, opack, recv_opack, recv_ocorner, face_map, bands, uplift, level, k_hi, k_lo,
    load_sem, sec_send, sec_recv, blk_send, blk_recv, diag_send, diag_recv,
    up_send, up_recv, src_send, src_recv,
):
    n_sec = lax.axis_size("sec")
    n_blk = lax.axis_size("blk")
    sec = lax.axis_index("sec")
    blk = lax.axis_index("blk")
    thick, rows, lanes = slab.shape[1:]
    ext_rows = ext.shape[2]
    ocols = ocean.shape[2]
    oext_cols = oext.shape[2]
    dip = face_map.shape[1]
    tile_cols = bands.shape[1]
    front, back = pl.ds(0, FRONT), pl.ds(FRONT, thick - FRONT)

    def has_sec(step):
        return sec + step < n_sec if step > 0 else sec + step >= 0

    def has_blk(step):
        return blk + step < n_blk if step > 0 else blk + step >= 0

    own_rows, own_lanes = pl.ds(0, rows), pl.ds(0, lanes)
    ocean_rows, ocean_cols = pl.ds(OHALO, rows), pl.ds(0, ocols)
    loads = []
    for part, layers in ((front, pl.ds(1, FRONT)), (back, pl.ds(1 + FRONT, thick - FRONT))):
        loads += [
            (slab.at[:, part], ext.at[pl.ds(0, FIELDS), layers, own_rows, own_lanes]),
            (buoyancy.at[part], ext.at[BUO, layers, own_rows, own_lanes]),
            (lame_lambda.at[part], ext.at[LAM, layers, own_rows, own_lanes]),
            (lame_mu.at[part], ext.at[MU, layers, own_rows, own_lanes]),
        ]
    loads += [
        (face_hbm, face_map),
        (bands_hbm, bands),
        (ocean, oext.at[pl.ds(0, 3), ocean_rows, ocean_cols]),
        (depth, oext.at[3, ocean_rows, ocean_cols]),
    ]
    loads = [pltpu.make_async_copy(src, dst, load_sem.at[i]) for i, (src, dst) in enumerate(loads)]
    for load in loads:
        load.start()

    recv_rows[...] = jnp.zeros_like(recv_rows)
    recv_pack[...] = jnp.zeros_like(recv_pack)
    recv_corner[...] = jnp.zeros_like(recv_corner)
    recv_opack[...] = jnp.zeros_like(recv_opack)
    recv_ocorner[...] = jnp.zeros_like(recv_ocorner)
    for first in (0, OHALO + rows):
        level[first:first + OHALO, :] = jnp.zeros((OHALO, oext_cols), jnp.float32)
        oext[:, first:first + OHALO, 0:ocols] = jnp.zeros((4, OHALO, ocols), jnp.float32)

    barrier = pltpu.get_barrier_semaphore()

    def greet(step, turn):
        pl.semaphore_signal(
            barrier, inc=1,
            device_id=(sec + step, lax.rem(blk + turn, n_blk)), device_id_type=MESH,
        )

    for turn in range(1, n_blk):
        greet(0, turn)
    for step in SEC_DIRS:
        @pl.when(has_sec(step))
        def _():
            for turn in range(n_blk):
                greet(step, turn)

    for f in range(FIELDS):
        ext[f, 0] = jnp.zeros(ext.shape[2:], jnp.float32)
        ext[f, thick + 1] = jnp.zeros(ext.shape[2:], jnp.float32)

    def remote(src, dst, send_sem, recv_sem, target):
        return pltpu.make_async_remote_copy(
            src_ref=src, dst_ref=dst, send_sem=send_sem, recv_sem=recv_sem,
            device_id=target, device_id_type=MESH)

    def sec_copy(d, i):
        out_rows = pl.ds(rows, OHALO) if d == 0 else pl.ds(OHALO, OHALO)
        to_rows = pl.ds(0, OHALO) if d == 0 else pl.ds(OHALO + rows, OHALO)
        if i == 2:
            fluxes = pl.ds(1, 3)
            src, dst = oext.at[fluxes, out_rows, ocean_cols], oext.at[fluxes, to_rows, ocean_cols]
        else:
            part = pl.ds(0, part_rows(d, (FRONT, thick - FRONT)[i]))
            src, dst = send_rows.at[d, i, part], recv_rows.at[d, i, part]
        return remote(src, dst, sec_send.at[d, i], sec_recv.at[d, i], (sec + SEC_DIRS[d], blk))

    def blk_copy(e, i):
        if i == 2:
            src, dst = opack, recv_opack.at[e]
        else:
            part = (front, back)[i]
            src, dst = pack.at[part], recv_pack.at[e, part]
        return remote(src, dst, blk_send.at[e, i], blk_recv.at[e, i], (sec, blk + SEC_DIRS[e]))

    def diag_copy(d, e, i):
        if i == 2:
            src = opack.at[pl.ds(rows - OHALO, OHALO) if d == 0 else pl.ds(0, OHALO)]
            dst = recv_ocorner.at[d, e]
        else:
            part = (front, back)[i]
            src, dst = send_corner.at[d, part], recv_corner.at[d, e, part]
        return remote(src, dst, diag_send.at[d, e, i], diag_recv.at[d, e, i],
                      (sec + SEC_DIRS[d], blk + SEC_DIRS[e]))

    def both(d, e):
        return jnp.logical_and(has_sec(SEC_DIRS[d]), has_blk(SEC_DIRS[e]))

    def from_both(d, e):
        return jnp.logical_and(has_sec(-SEC_DIRS[d]), has_blk(-SEC_DIRS[e]))

    def send_all(i):
        for d in range(2):
            @pl.when(has_sec(SEC_DIRS[d]))
            def _():
                sec_copy(d, i).start()
        for d in range(2):
            for e in range(2):
                @pl.when(both(d, e))
                def _():
                    diag_copy(d, e, i).start()
        for e in range(2):
            @pl.when(has_blk(SEC_DIRS[e]))
            def _():
                blk_copy(e, i).start()

    def await_all(i):
        for d in range(2):
            @pl.when(has_sec(-SEC_DIRS[d]))
            def _():
                sec_copy(d, i).wait_recv()
            for e in range(2):
                @pl.when(from_both(d, e))
                def _():
                    diag_copy(d, e, i).wait_recv()
        for e in range(2):
            @pl.when(has_blk(-SEC_DIRS[e]))
            def _():
                blk_copy(e, i).wait_recv()

    lane = lax.broadcasted_iota(jnp.int32, (rows, lanes), 1)

    def pack_layer(t):
        packed = jnp.zeros((rows, lanes), jnp.float32)
        for f in range(ALL):
            value = ext[f, t + 1, 0:rows, 0:lanes]
            moved = pltpu.roll(value, 4 * f, 1) if f else value
            packed = jnp.where(((lane - 4 * f + 2) & (lanes - 1)) < 4, moved, packed)
        i = 0 if t < FRONT else 1
        for f, count, at in row_pieces(0, t):
            send_rows[0, i, at:at + count, :] = ext[f, t + 1, rows - count:rows, 0:lanes]
        for f, count, at in row_pieces(1, t):
            send_rows[1, i, at:at + count, :] = ext[f, t + 1, 0:count, 0:lanes]
        pack[t] = packed
        send_corner[0, t] = packed[rows - HALO:, :]
        send_corner[1, t] = packed[0:HALO, :]

    for load in loads[:4]:
        load.wait()
    for t in range(FRONT):
        pack_layer(t)
    near = (n_blk - 1) + sum(jnp.where(has_sec(step), n_blk, 0) for step in SEC_DIRS)
    pl.semaphore_wait(barrier, near)
    send_all(0)
    for load in loads[4:8]:
        load.wait()
    for t in range(FRONT, thick):
        pack_layer(t)
    send_all(1)

    for load in loads[8:]:
        load.wait()
    opacked = jnp.zeros((rows, lanes), jnp.float32)
    for a in range(4):
        value = oext[a, OHALO:OHALO + rows, 0:ocols]
        edges = jnp.where(lane < lanes // 2, value[:, 0:lanes], value[:, ocols - lanes:])
        moved = pltpu.roll(edges, 16 * a, 1) if a else edges
        opacked = jnp.where(((lane - 16 * a + 8) & (lanes - 1)) < 16, moved, opacked)
    opack[...] = opacked
    send_all(2)

    def width_at(step):
        total = jnp.zeros((1, 1), jnp.float32)
        for j in range(tile_cols):
            total = jnp.where(blk + step == j, bands[0:1, j:j + 1].astype(jnp.float32), total)
        return jnp.maximum(total, 1.0)

    chunk = 32
    face = face_map[...].astype(jnp.float32)
    index = lax.broadcasted_iota(jnp.int32, (chunk, dip), 0).astype(jnp.float32)
    own_column = (blk * ocols).astype(jnp.float32)

    def fill(first, column, count, width):
        distance = jnp.abs((index[0:count] + (own_column + float(column))) - face)
        decay = jnp.exp2(distance * (-math.pi / 2.0 * math.log2(math.e) / width))
        under = width + width * (decay * decay)
        guess = pl.reciprocal(under, approx=True)
        value = decay * (guess * (2.0 - under * guess))
        high = value.astype(jnp.bfloat16)
        k_hi[first:first + count, :] = high
        k_lo[first:first + count, :] = (value - high.astype(jnp.float32)).astype(jnp.bfloat16)

    here = width_at(0)
    for first in range(0, ocols, chunk):
        fill(first, first, chunk, here)
    fill(ocols, ocols, 16, width_at(1))
    fill(oext_cols - 16, -16, 16, width_at(-1))
    blank = jnp.zeros((oext_cols - ocols - 32, dip), jnp.bfloat16)
    k_hi[ocols + 16:oext_cols - 16, :] = blank
    k_lo[ocols + 16:oext_cols - 16, :] = blank

    picks = (lane & 3) < 2

    def assemble(t):
        ext_pack[t, 0:rows, :] = jnp.where(picks, recv_pack[1, t], recv_pack[0, t])
        few = picks[0:HALO]
        after, before = pl.ds(rows, HALO), pl.ds(ext_rows - HALO, HALO)
        ext_pack[t, after, :] = jnp.where(few, recv_corner[1, 1, t], recv_corner[1, 0, t])
        ext_pack[t, before, :] = jnp.where(few, recv_corner[0, 1, t], recv_corner[0, 0, t])
        sides = ext_pack[t]
        for f in range(ALL):
            ext[f, t + 1, :, lanes:2 * lanes] = (
                pltpu.roll(sides, lanes - 4 * f, 1) if f else sides)
        i = 0 if t < FRONT else 1
        for f, count, at in row_pieces(0, t):
            ext[f, t + 1, ext_rows - count:ext_rows, 0:lanes] = recv_rows[0, i, at:at + count, :]
        for f, count, at in row_pieces(1, t):
            ext[f, t + 1, rows:rows + count, 0:lanes] = recv_rows[1, i, at:at + count, :]

    def velocity_1(u, s11, s11_next, s12, s13):
        return ext[V1, u] + time_step * ext[BUO, u] * (
            (s11_next - s11) + (s12 - rows_down(s12)) + (s13 - lanes_down(s13)))

    def velocity(t):
        u = t + 1
        s12, s13, s23 = ext[S12, u], ext[S13, u], ext[S23, u]
        scale = time_step * ext[BUO, u]
        s22, s33 = ext[S22, u], ext[S33, u]
        ext[V1, u] = velocity_1(u, ext[S11, u], ext[S11, u + 1], s12, s13)
        ext[V2, u] = ext[V2, u] + scale * (
            (rows_up(s22) - s22) + (s12 - ext[S12, u - 1]) + (s23 - lanes_down(s23)))
        ext[V3, u] = ext[V3, u] + scale * (
            (lanes_up(s33) - s33) + (s13 - ext[S13, u - 1]) + (s23 - rows_down(s23)))

    def strains(u):
        v1, v2, v3 = ext[V1, u], ext[V2, u], ext[V3, u]
        return v1 - ext[V1, u - 1], v2 - rows_down(v2), v3 - lanes_down(v3)

    def stress_values(u):
        v1, v2, v3 = ext[V1, u], ext[V2, u], ext[V3, u]
        e1, e2, e3 = strains(u)
        scale = time_step * ext[MU, u]
        common = time_step * ext[LAM, u] * (e1 + e2 + e3)
        twice = 2.0 * scale
        return (
            (S11, ext[S11, u] + (common + twice * e1)),
            (S22, ext[S22, u] + (common + twice * e2)),
            (S33, ext[S33, u] + (common + twice * e3)),
            (S23, ext[S23, u] + scale * ((lanes_up(v2) - v2) + (rows_up(v3) - v3))),
            (S13, ext[S13, u] + scale * ((lanes_up(v1) - v1) + (ext[V3, u + 1] - v3))),
            (S12, ext[S12, u] + scale * ((rows_up(v1) - v1) + (ext[V2, u + 1] - v2))),
        )

    def stress(t):
        for f, value in stress_values(t + 1):
            ext[f, t + 1] = value

    def last_stress(t):
        for f in (V1, V2, V3):
            slab_out[f, t] = ext[f, t + 1, 0:rows, 0:lanes]
        for f, value in stress_values(t + 1):
            slab_out[f, t] = value[0:rows, 0:lanes]

    await_all(0)
    for t in range(FRONT):
        assemble(t)
    velocity(0)
    velocity(1)
    stress(0)
    e1, e2, e3 = strains(2)
    s11_next = ext[S11, 2] + time_step * (
        ext[LAM, 2] * (e1 + e2 + e3) + 2.0 * ext[MU, 2] * e1)
    second = velocity_1(1, ext[S11, 1], s11_next, ext[S12, 1], ext[S13, 1])
    rise = time_step * (ext[V1, 1] + second)
    uplift[blk] = rise[0:rows, 0:lanes]

    def up_copy(turn):
        return remote(uplift.at[blk], uplift.at[blk], up_send.at[turn], up_recv.at[turn],
                      (sec, lax.rem(blk + turn, n_blk)))

    def up_arrival(turn):
        owner = lax.rem(blk + n_blk - turn, n_blk)
        return remote(uplift.at[owner], uplift.at[owner], up_send.at[turn], up_recv.at[turn],
                      (sec, lax.rem(blk + turn, n_blk)))

    for turn in range(1, n_blk):
        up_copy(turn).start()

    for e in range(2):
        @pl.when(has_blk(-SEC_DIRS[e]))
        def _():
            blk_copy(e, 2).wait_recv()
    for turn in range(1, n_blk):
        up_arrival(turn).wait_recv()
    whole = jnp.concatenate([uplift[b] for b in range(n_blk)], axis=1)
    high = whole.astype(jnp.bfloat16)
    low = (whole - high.astype(jnp.float32)).astype(jnp.bfloat16)
    dims = (((1,), (1,)), ((), ()))
    by_high = lax.dot_general(jnp.concatenate([high, low], axis=0), k_hi[...], dims,
                              preferred_element_type=jnp.float32)
    by_low = lax.dot_general(high, k_lo[...], dims, preferred_element_type=jnp.float32)
    own_source = by_high[0:rows] + (by_high[rows:] + by_low)
    right = (lane & 15) < 8
    beside = jnp.where(right, recv_opack[1], recv_opack[0])
    level[OHALO:OHALO + rows, 0:ocols] = oext[0, ocean_rows, ocean_cols] + own_source[:, 0:ocols]
    level[OHALO:OHALO + rows, ocols:] = beside + own_source[:, ocols:]

    def src_copy(d):
        out_rows = pl.ds(rows, OHALO) if d == 0 else pl.ds(OHALO, OHALO)
        to_rows = pl.ds(0, OHALO) if d == 0 else pl.ds(OHALO + rows, OHALO)
        return remote(level.at[out_rows], level.at[to_rows], src_send.at[d], src_recv.at[d],
                      (sec + SEC_DIRS[d], blk))

    for d in range(2):
        @pl.when(has_sec(SEC_DIRS[d]))
        def _():
            src_copy(d).start()

    await_all(1)
    for t in range(FRONT, thick):
        assemble(t)
    for t in range(2, thick):
        velocity(t)
    for t in range(1, thick):
        stress(t)

    for t in range(thick):
        velocity(t)
    for t in range(thick):
        last_stress(t)

    for d in range(2):
        @pl.when(has_sec(-SEC_DIRS[d]))
        def _():
            sec_copy(d, 2).wait_recv()
        for e in range(2):
            @pl.when(from_both(d, e))
            def _():
                diag_copy(d, e, 2).wait_recv()
    for d in range(2):
        @pl.when(has_sec(-SEC_DIRS[d]))
        def _():
            src_copy(d).wait_recv()

    side_rows = jnp.concatenate([
        jnp.where(right[0:OHALO], recv_ocorner[0, 1], recv_ocorner[0, 0]),
        beside,
        jnp.where(right[0:OHALO], recv_ocorner[1, 1], recv_ocorner[1, 0]),
    ], axis=0)
    ocean_out[0] = level[...]
    for a in range(1, 4):
        ocean_out[a, :, 0:ocols] = oext[a, :, 0:ocols]
        ocean_out[a, :, ocols:] = pltpu.roll(side_rows, lanes - 16 * a, 1)

    for d in range(2):
        @pl.when(has_sec(SEC_DIRS[d]))
        def _():
            for i in range(3):
                sec_copy(d, i).wait_send()
            src_copy(d).wait_send()
        for e in range(2):
            @pl.when(both(d, e))
            def _():
                for i in range(3):
                    diag_copy(d, e, i).wait_send()
    for e in range(2):
        @pl.when(has_blk(SEC_DIRS[e]))
        def _():
            for i in range(3):
                blk_copy(e, i).wait_send()
    for turn in range(1, n_blk):
        up_copy(turn).wait_send()


def wave_body(slab, state, slab_out, ocean_out, result, slab_sem, ocean_sem):
    n_sec = lax.axis_size("sec")
    n_blk = lax.axis_size("blk")
    sec = lax.axis_index("sec")
    blk = lax.axis_index("blk")
    rows, ocols = result.shape[1:]
    all_rows, oext_cols = state.shape[1:]
    slab_copy = pltpu.make_async_copy(slab, slab_out, slab_sem)
    slab_copy.start()
    surface, flux_strike, flux_dip, still = (state[a] for a in range(4))
    row_at = lax.broadcasted_iota(jnp.int32, (all_rows, oext_cols), 0) + (sec * rows - OHALO)
    col = lax.broadcasted_iota(jnp.int32, (all_rows, oext_cols), 1)
    col_at = jnp.where(col < (ocols + oext_cols) // 2, col, col - oext_cols) + blk * ocols
    wet = ((row_at >= 0) & (row_at < n_sec * rows)) & ((col_at >= 0) & (col_at < n_blk * ocols))
    surface = jnp.where(wet, surface, 0.0)
    pull = wave_step * 0.5 * still
    for _ in range(WAVE_STEPS):
        change = (rows_up(flux_strike) - rows_down(flux_strike)) + (
            lanes_up(flux_dip) - lanes_down(flux_dip))
        surface = jnp.where(wet, surface - wave_step * 0.5 * change, 0.0)
        flux_strike = flux_strike - pull * (rows_up(surface) - rows_down(surface))
        flux_dip = flux_dip - pull * (lanes_up(surface) - lanes_down(surface))
    for a, value in enumerate((surface, flux_strike, flux_dip)):
        result[a] = value[OHALO:OHALO + rows, 0:ocols]
    ocean_copy = pltpu.make_async_copy(result, ocean_out, ocean_sem)
    ocean_copy.start()
    slab_copy.wait()
    ocean_copy.wait()


def on_device(
    slab_state, buoyancy, lame_lambda, lame_mu, face_map, band_widths, ocean_state, water_depth
):
    n_blk = lax.axis_size("blk")
    thick, rows, lanes = slab_state.shape[1:]
    ocols = ocean_state.shape[2]
    dip = face_map.shape[0]
    ext_rows = rows + 8
    oext_cols = ocols + lanes
    max_rows = max(part_rows(d, n) for d in range(2) for n in (FRONT, thick - FRONT))
    f32 = jnp.float32
    vmem = pl.BlockSpec(memory_space=pltpu.VMEM)
    hbm = pl.BlockSpec(memory_space=pltpu.HBM)
    dma = pltpu.SemaphoreType.DMA
    slab_done, state = pl.pallas_call(
        kernel_body,
        out_shape=(
            jax.ShapeDtypeStruct(slab_state.shape, f32),
            jax.ShapeDtypeStruct((4, rows + 2 * OHALO, oext_cols), f32),
        ),
        in_specs=[hbm] * 8,
        out_specs=(vmem, vmem),
        scratch_shapes=[
            pltpu.VMEM((ALL, thick + 2, ext_rows, 2 * lanes), f32),
            pltpu.VMEM((2, 2, max_rows, lanes), f32),
            pltpu.VMEM((2, 2, max_rows, lanes), f32),
            pltpu.VMEM((thick, rows, lanes), f32),
            pltpu.VMEM((2, thick, rows, lanes), f32),
            pltpu.VMEM((2, thick, HALO, lanes), f32),
            pltpu.VMEM((2, 2, thick, HALO, lanes), f32),
            pltpu.VMEM((thick, ext_rows, lanes), f32),
            pltpu.VMEM((4, rows + 2 * OHALO, oext_cols), f32),
            pltpu.VMEM((rows, lanes), f32),
            pltpu.VMEM((2, rows, lanes), f32),
            pltpu.VMEM((2, 2, OHALO, lanes), f32),
            pltpu.VMEM((1, dip), jnp.int32),
            pltpu.VMEM(band_widths.shape, jnp.int32),
            pltpu.VMEM((n_blk, rows, lanes), f32),
            pltpu.VMEM((rows + 2 * OHALO, oext_cols), f32),
            pltpu.VMEM((oext_cols, dip), jnp.bfloat16),
            pltpu.VMEM((oext_cols, dip), jnp.bfloat16),
            dma((12,)),
            dma((2, 3)), dma((2, 3)),
            dma((2, 3)), dma((2, 3)),
            dma((2, 2, 3)), dma((2, 2, 3)),
            dma((n_blk,)), dma((n_blk,)),
            dma((2,)), dma((2,)),
        ],
        compiler_params=pltpu.CompilerParams(
            collective_id=0, has_side_effects=True, vmem_limit_bytes=32 * 1024 * 1024
        ),
        cost_estimate=pl.CostEstimate(
            flops=200_000_000, bytes_accessed=2_000_000, transcendentals=500_000),
    )(
        *(pltpu.with_memory_space_constraint(x, pltpu.HBM) for x in (
            slab_state, buoyancy, lame_lambda, lame_mu, face_map.reshape(1, dip), band_widths,
            ocean_state, water_depth))
    )
    return pl.pallas_call(
        wave_body,
        out_shape=(
            jax.ShapeDtypeStruct(slab_state.shape, f32),
            jax.ShapeDtypeStruct(ocean_state.shape, f32),
        ),
        in_specs=[pl.BlockSpec(memory_space=pl.ANY), vmem],
        out_specs=(hbm, hbm),
        scratch_shapes=[pltpu.VMEM(ocean_state.shape, f32), dma, dma],
        compiler_params=pltpu.CompilerParams(vmem_limit_bytes=16 * 1024 * 1024),
    )(slab_done, state)


def solution(mesh):
    in_specs = (
        P(None, None, "sec", "blk"),
        P(None, "sec", "blk"),
        P(None, "sec", "blk"),
        P(None, "sec", "blk"),
        P(),
        P("sec", None),
        P(None, "sec", "blk"),
        P("sec", "blk"),
    )
    out_specs = (P(None, None, "sec", "blk"), P(None, "sec", "blk"))
    return jax.shard_map(
        on_device, mesh=mesh, in_specs=in_specs, out_specs=out_specs, check_vma=False
    )
```
